32 devices in a mesh: dp: 4 (over y, core), seq: 8 (over z, x).
Axes of the slice: x: 2, y: 2, z: 4, core: 2. Of those that a mesh axis runs over, the one named last changes fastest.
Arguments:
- inputs: bfloat16 [4, 2048, 1024], P('dp', 'seq'), may hold values from -6 to 6
- cotangent: bfloat16 [4, 2048, 1024], P('dp', 'seq'), may hold values from -6 to 6
- context: int32 [4], P('dp'), may hold values from 1 to 7
- levels: int32 [4, 8], P('dp', 'seq'), may hold values from 1 to 999
- w_qkv: bfloat16 [1024, 3072], P(('dp', 'seq')), may hold values from -0.1875 to 0.1875
- b_qkv: bfloat16 [3072], P(('dp', 'seq')), may hold values from -3 to 3
- w_out: bfloat16 [1024, 1024], P(('dp', 'seq')), may hold values from -3 to 3
- b_out: bfloat16 [1024], P(('dp', 'seq')), may hold values from -3 to 3
- w_up: bfloat16 [1024, 4096], P(('dp', 'seq')), may hold values from -0.1875 to 0.1875
- b_up: bfloat16 [4096], P(('dp', 'seq')), may hold values from -3 to 3
- w_down: bfloat16 [4096, 1024], P(('dp', 'seq')), may hold values from -0.09375 to 0.09375
- b_down: bfloat16 [1024], P(('dp', 'seq')), may hold values from -3 to 3
- w_mod: bfloat16 [1024, 6144], P(('dp', 'seq')), may hold values from -0.1875 to 0.1875
- b_mod: bfloat16 [6144], P(('dp', 'seq')), may hold values from -3 to 3
Outputs:
- layer_out: bfloat16 [4, 2048, 1024], P('dp', 'seq')
- input_grad: bfloat16 [4, 2048, 1024], P('dp', 'seq')
- g_wqkv: float32 [1024, 3072], P(('dp', 'seq'))
- g_bqkv: float32 [3072], P(('dp', 'seq'))
- g_wout: float32 [1024, 1024], P(('dp', 'seq'))
- g_bout: float32 [1024], P(('dp', 'seq'))
- g_wup: float32 [1024, 4096], P(('dp', 'seq'))
- g_bup: float32 [4096], P(('dp', 'seq'))
- g_wdown: float32 [4096, 1024], P(('dp', 'seq'))
- g_bdown: float32 [1024], P(('dp', 'seq'))
- g_wmod: float32 [1024, 6144], P(('dp', 'seq'))
- g_bmod: float32 [6144], P(('dp', 'seq'))
The draws below stay inside these ranges and needn't reach their ends.
All inputs are finite; a program needn't handle non-finite values.
Results may differ from the reference program's by a relative error of at most 0.017.
Values may be sent and summed in bfloat16 or wider, within the bound.
No kernel may reach another device: no remote copies, remote signals or barrier semaphores. Data moves between devices by JAX's collectives and lax.ppermute only.
A program may use at most 256 MiB of HBM per device.

```python
import math
import jax
import jax.numpy as jnp
from jax import lax

D = 1024
H = 16
HD = 64
FF = 4096
PW = 16
P_SIZE = 256
LEVELS = 1000
FRAMES = 8
CLIPS = 4
S = 2048


def set_ends(values, key, smallest, largest):
    shape = values.shape
    index_at = [jax.random.randint(jax.random.fold_in(key, axis), (), 0, shape[axis]) for axis in range(len(shape))]
    values = values.at[tuple(index_at)].set(smallest)
    longest = shape.index(max(shape))
    index_at[longest] = (index_at[longest] + 1) % shape[longest]
    return values.at[tuple(index_at)].set(largest)


def steps_of(stream_key, extent, pieces, least, high):
    def one(dim, blocks):
        heights = jax.random.uniform(jax.random.fold_in(jax.random.fold_in(stream_key, 6), dim), (blocks,), jnp.float32, least / len(pieces), high / len(pieces))
        return jnp.repeat(jnp.exp(heights), extent[dim] // blocks).reshape((-1,) + (1,) * (len(extent) - dim - 1))

    loudness = one(*pieces[0])
    for cut in pieces[1:]:
        loudness = loudness * one(*cut)
    return loudness


def gaussian(stream_key, shape, scale, limit, pieces=(), held_as=jnp.bfloat16):
    level = steps_of(stream_key, shape, pieces, -0.22, 0.18) if pieces else 1.0
    values = jax.random.normal(stream_key, shape, jnp.float32) * scale * level
    return jnp.minimum(jnp.maximum(values, -limit), limit).astype(held_as)


def setup_inputs(seed: int = 0) -> dict:
    key_list = jax.random.split(jax.random.key(seed), 15)
    inputs = gaussian(key_list[0], (CLIPS, S, D), 1.0, 6.0, ((0, 4), (1, 8)))
    cotangent = gaussian(key_list[1], (CLIPS, S, D), 1.0, 6.0, ((0, 4), (1, 8)))
    context = set_ends(jax.random.randint(key_list[2], (CLIPS,), 1, FRAMES), jax.random.fold_in(key_list[2], 1), 1, FRAMES - 1).astype(jnp.int32)
    levels = set_ends(jax.random.randint(key_list[3], (CLIPS, FRAMES), 1, LEVELS), jax.random.fold_in(key_list[3], 1), 1, LEVELS - 1).astype(jnp.int32)
    w_qkv = gaussian(key_list[4], (D, 3 * D), D ** -0.5, 0.1875, ((0, 32),))
    b_qkv = gaussian(key_list[5], (3 * D,), 0.5, 3.0, ((0, 32),))
    w_out = gaussian(key_list[6], (D, D), (max(1, D * 8 // (FRAMES * P_SIZE))) ** -0.5, 3.0, ((0, 32),))
    b_out = gaussian(key_list[7], (D,), 0.5, 3.0, ((0, 32),))
    w_up = gaussian(key_list[8], (D, FF), D ** -0.5, 0.1875, ((0, 32),))
    b_up = gaussian(key_list[9], (FF,), 0.5, 3.0, ((0, 32),))
    w_down = gaussian(key_list[10], (FF, D), FF ** -0.5, 0.09375, ((0, 32),))
    b_down = gaussian(key_list[11], (D,), 0.5, 3.0, ((0, 32),))
    w_mod = gaussian(key_list[12], (D, 6 * D), D ** -0.5, 0.1875, ((0, 32),))
    b_mod = gaussian(key_list[13], (6 * D,), 0.5, 3.0, ((0, 32),))
    return dict(inputs=inputs, cotangent=cotangent, context=context, levels=levels, w_qkv=w_qkv, b_qkv=b_qkv, w_out=w_out, b_out=b_out, w_up=w_up, b_up=b_up, w_down=w_down, b_down=b_down, w_mod=w_mod, b_mod=b_mod)


@jax.custom_vjp
def low(v):
    return lax.optimization_barrier(v.astype(jnp.bfloat16)).astype(jnp.float32)

@jax.custom_vjp
def low_back(v):
    return v

def low_keep(v):
    return (low(v), None)

def low_pass(kept, grad):
    return (grad,)

def back_keep(v):
    return (v, None)

def back_low(kept, grad):
    return (low(grad),)
low.defvjp(low_keep, low_pass)
low_back.defvjp(back_keep, back_low)
eps = 1e-06
highest = lax.Precision.HIGHEST

def layer_norm(values):
    row_mean = lax.optimization_barrier(jnp.mean(values, axis=-1, keepdims=True))
    centred = values - row_mean
    return centred * lax.rsqrt(lax.optimization_barrier(jnp.mean(centred * centred, axis=-1, keepdims=True)) + eps)

def level_embedding(effective, width):
    half_width = width // 2
    frequency = jnp.exp(-math.log(10000.0) * jnp.arange(half_width).astype(jnp.float32) / half_width)
    angles = effective.astype(jnp.float32)[..., None] * frequency
    return jnp.concatenate([jnp.cos(angles), jnp.sin(angles)], axis=-1)

def rope_angles(frame_pos, row_pos, column_pos, head_width):
    pair_count = head_width // 2
    time_pairs = head_width // 8
    space_pairs = 3 * head_width // 16
    pair_index = jnp.arange(pair_count)
    axis_pick = jnp.where(pair_index < time_pairs, 0, jnp.where(pair_index < time_pairs + space_pairs, 1, 2))
    local_rank = jnp.where(axis_pick == 0, pair_index, jnp.where(axis_pick == 1, pair_index - time_pairs, pair_index - time_pairs - space_pairs))
    group_size = jnp.where(axis_pick == 0, time_pairs, space_pairs)
    frequency = jnp.exp(-math.log(10000.0) * local_rank.astype(jnp.float32) / group_size.astype(jnp.float32))
    position = jnp.where(axis_pick == 0, frame_pos[:, None], jnp.where(axis_pick == 1, row_pos[:, None], column_pos[:, None]))
    return position.astype(jnp.float32) * frequency

def rotate(values, cosine, sine_table):
    half_width = values.shape[-1] // 2
    first_half = values[..., :half_width]
    second_half = values[..., half_width:]
    cos_b = cosine[:, None, :]
    sin_b = sine_table[:, None, :]
    return jnp.concatenate([first_half * cos_b - second_half * sin_b, first_half * sin_b + second_half * cos_b], axis=-1)

def clip_forward(inputs, clip_levels, clip_context, w_qkv, b_qkv, w_out, b_out, w_up, b_up, w_down, b_down, w_mod, b_mod):
    frame_of = jnp.arange(FRAMES)
    effective = jnp.where(frame_of < clip_context, 0, clip_levels)
    condition = low(jax.nn.silu(level_embedding(effective, D)))
    modulation = low_back(jnp.dot(condition, w_mod, precision=highest, preferred_element_type=jnp.float32) + b_mod)
    shift_attend, scale_attend, gate_attend, shift_feed, scale_feed, gate_feed = jnp.split(modulation[:, None, :], 6, axis=-1)
    framed = inputs.reshape(FRAMES, P_SIZE, D)
    hidden = low((layer_norm(framed) * (1.0 + scale_attend) + shift_attend).reshape(S, D))
    qkv_rows = low_back(jnp.dot(hidden, w_qkv, precision=highest, preferred_element_type=jnp.float32) + b_qkv)
    query_raw = qkv_rows[:, :D].reshape(S, H, HD)
    key_raw = qkv_rows[:, D:2 * D].reshape(S, H, HD)
    value_raw = qkv_rows[:, 2 * D:].reshape(S, H, HD)
    token_index = jnp.arange(S)
    frame_index = token_index // P_SIZE
    patch_index = token_index % P_SIZE
    angles = rope_angles(frame_index, patch_index // PW, patch_index % PW, HD)
    cosine = jnp.cos(angles)
    sine_table = jnp.sin(angles)
    queries = low(rotate(query_raw, cosine, sine_table))
    keys_low = low(rotate(key_raw, cosine, sine_table))
    values_low = low(value_raw)
    score_scale = 1.0 / math.sqrt(HD)
    allowed = frame_index[:, None] >= frame_index[None, :]

    def head_attention(parts):
        query_head, key_head, value_head = parts
        scores = low_back(jnp.dot(query_head, key_head.T, precision=highest, preferred_element_type=jnp.float32) * score_scale)
        scores = jnp.where(allowed, scores, -1e+30)
        probs = low(jax.nn.softmax(scores, axis=-1))
        return jnp.dot(probs, value_head, precision=highest, preferred_element_type=jnp.float32)
    per_head = lax.map(jax.checkpoint(head_attention), (jnp.transpose(queries, (1, 0, 2)), jnp.transpose(keys_low, (1, 0, 2)), jnp.transpose(values_low, (1, 0, 2))))
    attended = low_back(low(jnp.transpose(per_head, (1, 0, 2)).reshape(S, D)))
    branch = low_back(jnp.dot(attended, w_out, precision=highest, preferred_element_type=jnp.float32) + b_out).reshape(FRAMES, P_SIZE, D)
    middle = framed + gate_attend * branch
    hidden_mid = low((layer_norm(middle) * (1.0 + scale_feed) + shift_feed).reshape(S, D))
    up_rows = low_back(jnp.dot(hidden_mid, w_up, precision=highest, preferred_element_type=jnp.float32) + b_up)
    activated = low(jax.nn.gelu(up_rows, approximate=True))
    down_rows = low_back(jnp.dot(activated, w_down, precision=highest, preferred_element_type=jnp.float32) + b_down).reshape(FRAMES, P_SIZE, D)
    return (middle + gate_feed * down_rows).reshape(S, D)

def reference(inputs, cotangent, context, levels, w_qkv, b_qkv, w_out, b_out, w_up, b_up, w_down, b_down, w_mod, b_mod):
    weights = tuple((w.astype(jnp.float32) for w in (w_qkv, b_qkv, w_out, b_out, w_up, b_up, w_down, b_down, w_mod, b_mod)))

    def one_clip(totals, item):
        clip_inputs, clip_cot, clip_context, clip_levels = item

        def forward(values, *params):
            return clip_forward(values, clip_levels, clip_context, *params)
        result, pull = jax.vjp(forward, clip_inputs.astype(jnp.float32), *weights)
        live_rows = (jnp.arange(S) // P_SIZE >= clip_context).astype(jnp.float32)[:, None]
        grads = pull(clip_cot.astype(jnp.float32) * live_rows)
        totals = tuple((total + grad for total, grad in zip(totals, grads[1:])))
        return (totals, (result.astype(jnp.bfloat16), grads[0].astype(jnp.bfloat16)))
    initial = tuple((jnp.zeros(w.shape, jnp.float32) for w in weights))
    totals, (layer_out, input_grad) = lax.scan(one_clip, initial, (inputs, cotangent, context, levels))
    return (layer_out, input_grad, totals[0], totals[1], totals[2], totals[3], totals[4], totals[5], totals[6], totals[7], totals[8], totals[9])
```

```python
import math

import jax
import jax.numpy as jnp
from jax import lax
from jax.experimental import pallas as pl
from jax.experimental.pallas import tpu as pltpu
from jax.sharding import Mesh, PartitionSpec as P

D = 1024
H = 16
HD = 64
PW = 16
EPS = 1e-06

ALL = ("p", "c", "r", "q")
SEQ = ("r", "q")
bf16 = jnp.bfloat16
f32 = jnp.float32


def layer_norm(values):
    row_mean = jnp.mean(values, axis=-1, keepdims=True)
    centred = values - row_mean
    inv_std = lax.rsqrt(jnp.mean(centred * centred, axis=-1, keepdims=True) + EPS)
    return (centred * inv_std, inv_std)


def norm_back(normed, inv_std, normed_grad):
    first_mean = jnp.mean(normed_grad, axis=-1, keepdims=True)
    second_mean = jnp.mean(normed_grad * normed, axis=-1, keepdims=True)
    return inv_std * (normed_grad - first_mean - normed * second_mean)


def level_embedding(effective, width):
    half_width = width // 2
    frequency = jnp.exp(
        -math.log(10000.0) * jnp.arange(half_width).astype(f32) / half_width
    )
    angles = effective.astype(f32)[..., None] * frequency
    return jnp.concatenate([jnp.cos(angles), jnp.sin(angles)], axis=-1)


def rope_angles(frame_pos, row_pos, column_pos, head_width):
    pair_count = head_width // 2
    time_pairs = head_width // 8
    space_pairs = 3 * head_width // 16
    pair_index = jnp.arange(pair_count)
    axis_pick = jnp.where(
        pair_index < time_pairs, 0, jnp.where(pair_index < time_pairs + space_pairs, 1, 2)
    )
    local_rank = jnp.where(
        axis_pick == 0,
        pair_index,
        jnp.where(axis_pick == 1, pair_index - time_pairs, pair_index - time_pairs - space_pairs),
    )
    group_size = jnp.where(axis_pick == 0, time_pairs, space_pairs)
    frequency = jnp.exp(-math.log(10000.0) * local_rank.astype(f32) / group_size.astype(f32))
    position = jnp.where(
        axis_pick == 0,
        frame_pos[:, None],
        jnp.where(axis_pick == 1, row_pos[:, None], column_pos[:, None]),
    )
    return position.astype(f32) * frequency


def outer_sum(left, right):
    return lax.dot_general(
        left, right, (((0,), (0,)), ((), ())), preferred_element_type=f32
    )


def back_dot(grads, weight):
    return lax.dot_general(
        grads, weight, (((1,), (1,)), ((), ())), preferred_element_type=f32
    )


def nt(a, b):
    return lax.dot_general(a, b, (((1,), (1,)), ((), ())), preferred_element_type=f32)


def attend_kernel(block, heads, q_ref, k_ref, vt_ref, ot_ref, lse_ref):
    frame = pl.program_id(0)
    for h in range(heads):
        query = q_ref[h]

        def step(j, carry):
            top, total, acc = carry
            rows = pl.ds(pl.multiple_of(j * block, block), block)
            scores = nt(k_ref[h, rows, :], query)
            new_top = jnp.maximum(top, jnp.max(scores, axis=0, keepdims=True))
            shrink = jnp.exp(top - new_top)
            weights = jnp.exp(scores - new_top)
            total = total * shrink + jnp.sum(weights, axis=0, keepdims=True)
            acc = acc * shrink + jnp.dot(
                vt_ref[h, :, rows], weights.astype(bf16), preferred_element_type=f32
            )
            return new_top, total, acc

        top, total, acc = lax.fori_loop(
            0,
            frame + 1,
            step,
            (
                jnp.full((1, block), -1e30, f32),
                jnp.zeros((1, block), f32),
                jnp.zeros((HD, block), f32),
            ),
        )
        ot_ref[h] = acc / total
        lse_ref[h] = top + jnp.log(total)


def attend(queries, keys, values_t, block):
    heads, tokens, _ = queries.shape
    frames = tokens // block
    return pl.pallas_call(
        lambda *refs: attend_kernel(block, heads, *refs),
        grid=(frames,),
        in_specs=[
            pl.BlockSpec((heads, block, HD), lambda i: (0, i, 0)),
            pl.BlockSpec((heads, tokens, HD), lambda i: (0, 0, 0)),
            pl.BlockSpec((heads, HD, tokens), lambda i: (0, 0, 0)),
        ],
        out_specs=[
            pl.BlockSpec((heads, HD, block), lambda i: (0, 0, i)),
            pl.BlockSpec((heads, 1, block), lambda i: (0, 0, i)),
        ],
        out_shape=[
            jax.ShapeDtypeStruct((heads, HD, tokens), f32),
            jax.ShapeDtypeStruct((heads, 1, tokens), f32),
        ],
        compiler_params=pltpu.CompilerParams(vmem_limit_bytes=40 << 20),
    )(queries, keys, values_t)


def attend_back_kernel(
    block, heads, frames, q_ref, k_ref, kt_ref, v_ref, do_ref, ot_ref, lse_ref,
    dqt_ref, dk_ref, dv_ref, delta_ref,
):
    dqt_ref[...] = jnp.zeros_like(dqt_ref)
    for h in range(heads):
        for i in range(frames):
            rows = slice(i * block, (i + 1) * block)
            grad_t = jnp.transpose(do_ref[h, rows, :].astype(f32))
            delta_ref[h, :, rows] = jnp.sum(grad_t * ot_ref[h, :, rows], axis=0, keepdims=True)

    def key_step(j, _):
        keys_at = pl.ds(pl.multiple_of(j * block, block), block)
        for h in range(heads):
            key = k_ref[h, keys_at, :]
            key_t = kt_ref[h, :, keys_at]
            value = v_ref[h, keys_at, :]

            def query_step(i, carry):
                dk, dv = carry
                rows = pl.ds(pl.multiple_of(i * block, block), block)
                query = q_ref[h, rows, :]
                grad = do_ref[h, rows, :]
                probs = jnp.exp(nt(key, query) - lse_ref[h, :, rows])
                prob_grad = nt(value, grad)
                score_grad = (probs * (prob_grad - delta_ref[h, :, rows])).astype(bf16)
                dv = dv + jnp.dot(probs.astype(bf16), grad, preferred_element_type=f32)
                dk = dk + jnp.dot(score_grad, query, preferred_element_type=f32)
                dqt_ref[h, :, rows] += jnp.dot(key_t, score_grad, preferred_element_type=f32)
                return dk, dv

            zero = jnp.zeros((block, HD), f32)
            dk, dv = lax.fori_loop(j, frames, query_step, (zero, zero))
            dk_ref[h, keys_at, :] = dk
            dv_ref[h, keys_at, :] = dv
        return 0

    lax.fori_loop(0, frames, key_step, 0)


def attend_back(queries, keys, keys_t, values, grad, out_t, lse, block):
    heads, tokens, _ = queries.shape
    frames = tokens // block
    return pl.pallas_call(
        lambda *refs: attend_back_kernel(block, heads, frames, *refs),
        out_shape=[
            jax.ShapeDtypeStruct((heads, HD, tokens), f32),
            jax.ShapeDtypeStruct((heads, tokens, HD), f32),
            jax.ShapeDtypeStruct((heads, tokens, HD), f32),
        ],
        scratch_shapes=[pltpu.VMEM((heads, 1, tokens), f32)],
        compiler_params=pltpu.CompilerParams(vmem_limit_bytes=48 << 20),
    )(queries, keys, keys_t, values, grad, out_t, lse)


def swap(values, axis):
    return lax.ppermute(values, axis, [(0, 1), (1, 0)])


def pair_up(values, axis):
    other = swap(values, axis)
    first = lax.axis_index(axis) == 0
    return jnp.stack([jnp.where(first, values, other), jnp.where(first, other, values)])


def line_gather(values, axis, size):
    me = lax.axis_index(axis)
    whole = jnp.zeros((size,) + values.shape, values.dtype)
    whole = lax.dynamic_update_index_in_dim(whole, values, me, 0)
    up, down = values, values
    for step in range(1, size):
        up = lax.ppermute(up, axis, [(i, i + 1) for i in range(size - 1)])
        down = lax.ppermute(down, axis, [(i + 1, i) for i in range(size - 1)])
        low, high = jnp.maximum(me - step, 0), jnp.minimum(me + step, size - 1)
        whole = lax.dynamic_update_index_in_dim(
            whole, jnp.where(me >= step, up, whole[low]), low, 0
        )
        whole = lax.dynamic_update_index_in_dim(
            whole, jnp.where(me + step < size, down, whole[high]), high, 0
        )
    return whole


def line_scatter(parts, axis, size):
    me = lax.axis_index(axis)
    total = lax.dynamic_index_in_dim(parts, me, 0, keepdims=False).astype(f32)
    for shift in range(1, size):
        mine = lax.dynamic_index_in_dim(parts, (me + shift) % size, 0, keepdims=False)
        total = total + lax.ppermute(
            mine.astype(bf16), axis, [(i, (i + shift) % size) for i in range(size)]
        ).astype(f32)
    return total


def chip_scatter(parts, sizes):
    half = parts.shape[-1] // 2
    one, two = parts[..., :half], parts[..., half:]
    one = line_scatter(jnp.moveaxis(one, 2, 0), "q", sizes["q"]).astype(bf16)
    two = line_scatter(two, "p", sizes["p"]).astype(bf16)
    one = line_scatter(one, "p", sizes["p"])
    two = line_scatter(jnp.moveaxis(two, 1, 0), "q", sizes["q"])
    both = jnp.concatenate([one, two], axis=-1).astype(bf16)
    return line_scatter(both, "r", sizes["r"])


def make_shards(sizes):
    seq = sizes["r"] * sizes["q"]
    dp = sizes["p"] * sizes["c"]
    devices = seq * dp
    heads = H // seq
    wide = heads * HD

    def spread(values, axes):
        return lax.all_to_all(values, axes, 0, 0, tiled=True)

    def shards(
        inputs, cotangent, context, levels, w_qkv, b_qkv, w_out, b_out, w_up, b_up,
        w_down, b_down, w_mod, b_mod,
    ):
        own_frame = lax.axis_index(SEQ)
        core = lax.axis_index("c")
        patches = inputs.shape[1]
        tokens = seq * patches
        own_rows = w_mod.shape[0]

        effective = jnp.where(own_frame < context, 0, levels[:, 0])
        condition = jax.nn.silu(level_embedding(effective, D)).astype(bf16)
        biases = jnp.concatenate([b_qkv, b_out, b_up, b_down, b_mod])
        first = jnp.concatenate(
            [
                condition.reshape(devices, own_rows),
                jnp.broadcast_to(biases, (devices, biases.shape[0])),
            ],
            axis=1,
        )
        first = spread(first, ALL)
        pieces = first[:, :own_rows]
        at = own_rows
        full = []
        for bias in (b_qkv, b_out, b_up, b_down, b_mod):
            size = bias.shape[0]
            full.append(first[:, at : at + size].reshape(-1).astype(f32))
            at += size
        qkv_bias, out_bias, up_bias, down_bias, mod_bias = full
        mod_parts = jnp.dot(pieces, w_mod, preferred_element_type=f32)
        modulation = jnp.sum(spread(mod_parts.astype(bf16), ALL).astype(f32), axis=0) + mod_bias
        shift_attend, scale_attend, gate_attend, shift_feed, scale_feed, gate_feed = jnp.split(
            modulation[None, :], 6, axis=-1
        )
        frame_mod = spread(jnp.broadcast_to(modulation[None, : 2 * D], (seq, 2 * D)), SEQ)

        own_qkv = jnp.transpose(w_qkv.reshape(own_rows, 3, seq, wide), (2, 0, 1, 3))
        own_qkv = jnp.broadcast_to(
            own_qkv.reshape(1, seq, own_rows, 3 * wide), (dp, seq, own_rows, 3 * wide)
        ).reshape(devices, own_rows, 3 * wide)
        own_qkv = spread(own_qkv, ALL).reshape(D, 3 * wide)

        def whole(weight):
            return lax.all_gather(weight, ALL, axis=0, tiled=True)

        out_weight, up_weight, down_weight = whole(w_out), whole(w_up), whole(w_down)
        qkv_weight = whole(w_qkv)

        rows = inputs[0]
        split = patches // 2
        part_a = line_gather(rows[:split], "r", sizes["r"])
        part_b = pair_up(rows[split:], "q")
        part_a = jnp.moveaxis(pair_up(part_a, "q"), 0, 1)
        part_b = line_gather(part_b, "r", sizes["r"])
        clip = jnp.concatenate([part_a, part_b], axis=2).reshape(seq, patches, D)

        clip_normed, _ = layer_norm(clip.astype(f32))
        hidden_all = (
            clip_normed * (1.0 + frame_mod[:, None, D:]) + frame_mod[:, None, :D]
        ).astype(bf16).reshape(tokens, D)
        own_bias = lax.dynamic_index_in_dim(
            qkv_bias.reshape(3, seq, wide), own_frame, 1, keepdims=False
        ).reshape(3 * wide)
        qkv_rows = jnp.dot(hidden_all, own_qkv, preferred_element_type=f32) + own_bias
        qkv_rows = jnp.transpose(qkv_rows.reshape(tokens, 3, heads, HD), (1, 2, 0, 3))
        token = jnp.arange(tokens)
        patch = token % patches
        angles = rope_angles(token // patches, patch // PW, patch % PW, HD)
        cosine, sine = jnp.cos(angles), jnp.sin(angles)
        cosine = jnp.concatenate([cosine, cosine], axis=-1)
        sine = jnp.concatenate([-sine, sine], axis=-1)

        def turn(values, way):
            turned = jnp.concatenate([values[..., HD // 2 :], values[..., : HD // 2]], axis=-1)
            return values * cosine + way * turned * sine

        score_scale = 1.0 / math.sqrt(HD)
        queries = (turn(qkv_rows[0], 1.0).astype(bf16) * score_scale).astype(bf16)
        keys = turn(qkv_rows[1], 1.0).astype(bf16)
        values = qkv_rows[2].astype(bf16)
        out_t, lse = attend(queries, keys, jnp.transpose(values, (0, 2, 1)), patches)

        attended = jnp.transpose(out_t.astype(bf16), (2, 0, 1)).reshape(seq, patches, wide)
        attended = jnp.transpose(spread(attended, SEQ), (1, 0, 2)).reshape(patches, D)

        start_rows = rows.astype(f32)
        branch = jnp.dot(attended, out_weight, preferred_element_type=f32) + out_bias
        middle = start_rows + gate_attend * branch
        normed_mid, inv_std_mid = layer_norm(middle)
        hidden_mid = (normed_mid * (1.0 + scale_feed) + shift_feed).astype(bf16)
        up_rows = jnp.dot(hidden_mid, up_weight, preferred_element_type=f32) + up_bias
        gelu_value, gelu_pull = jax.vjp(lambda u: jax.nn.gelu(u, approximate=True), up_rows)
        activated = gelu_value.astype(bf16)
        down_rows = jnp.dot(activated, down_weight, preferred_element_type=f32) + down_bias
        layer_out = middle + gate_feed * down_rows

        live = (own_frame >= context).astype(f32)[:, None]
        out_grad = cotangent[0].astype(f32) * live
        gate_feed_grad = jnp.sum(out_grad * down_rows, axis=0)
        down_grad = (out_grad * gate_feed).astype(bf16)
        g_bdown = jnp.sum(down_grad.astype(f32), axis=0)
        up_grad = gelu_pull(back_dot(down_grad, down_weight))[0].astype(bf16)
        g_bup = jnp.sum(up_grad.astype(f32), axis=0)
        hidden_mid_grad = back_dot(up_grad, up_weight)
        scale_feed_grad = jnp.sum(hidden_mid_grad * normed_mid, axis=0)
        shift_feed_grad = jnp.sum(hidden_mid_grad, axis=0)
        middle_grad = out_grad + norm_back(
            normed_mid, inv_std_mid, hidden_mid_grad * (1.0 + scale_feed)
        )
        gate_attend_grad = jnp.sum(middle_grad * branch, axis=0)
        branch_grad = (middle_grad * gate_attend).astype(bf16)
        g_bout = jnp.sum(branch_grad.astype(f32), axis=0)
        attended_grad = back_dot(branch_grad, out_weight).astype(bf16)

        grad_heads = jnp.transpose(attended_grad.reshape(patches, seq, wide), (1, 0, 2))
        grad_heads = spread(grad_heads, SEQ).reshape(tokens, heads, HD)
        grad_heads = jnp.transpose(grad_heads, (1, 0, 2))
        dq_t, dk, dv = attend_back(
            queries, keys, jnp.transpose(keys, (0, 2, 1)), values, grad_heads, out_t, lse, patches
        )
        dq = turn(jnp.transpose(dq_t, (0, 2, 1)) * score_scale, -1.0).astype(bf16)
        dk = turn(dk, -1.0).astype(bf16)
        dqkv = jnp.transpose(jnp.stack([dq, dk, dv.astype(bf16)]), (2, 0, 1, 3)).reshape(
            tokens, 3 * wide
        )
        qkv_grad = spread(dqkv.reshape(seq, patches, 3 * wide), SEQ)
        qkv_grad = jnp.transpose(
            qkv_grad.reshape(seq, patches, 3, wide), (1, 2, 0, 3)
        ).reshape(patches, 3 * D)
        g_bqkv = jnp.sum(qkv_grad.astype(f32), axis=0)
        hidden_grad = back_dot(qkv_grad, qkv_weight)
        normed, inv_std = layer_norm(start_rows)
        scale_attend_grad = jnp.sum(hidden_grad * normed, axis=0)
        shift_attend_grad = jnp.sum(hidden_grad, axis=0)
        input_grad = middle_grad + norm_back(
            normed, inv_std, hidden_grad * (1.0 + scale_attend)
        )

        g_own = outer_sum(hidden_all, dqkv).astype(bf16).reshape(devices, own_rows, 3 * wide)
        g_own = spread(g_own, ALL).reshape(dp, seq, own_rows, 3, wide)
        g_wqkv = jnp.transpose(jnp.sum(g_own.astype(f32), axis=0), (1, 2, 0, 3)).reshape(
            own_rows, 3 * D
        )

        def halves(values):
            return values.reshape(patches, sizes["p"], 2, -1)

        def shared(left, right):
            parted = halves(left)
            mine = lax.dynamic_index_in_dim(parted, core, 2, keepdims=False)
            theirs = lax.dynamic_index_in_dim(parted, 1 - core, 2, keepdims=False)
            mine = mine.reshape(patches, -1)
            got_left = swap(theirs.reshape(patches, -1), "c")
            got_right = swap(right, "c")
            total = outer_sum(
                jnp.concatenate([mine, got_left]), jnp.concatenate([right, got_right])
            ).astype(bf16)
            total = total.reshape(sizes["p"], sizes["r"], sizes["q"], -1, right.shape[1])
            return chip_scatter(total, sizes)

        g_wdown = shared(activated, down_grad)
        g_wup = shared(hidden_mid, up_grad)
        g_wout = shared(attended, branch_grad)

        mod_grad = jnp.concatenate(
            [
                shift_attend_grad, scale_attend_grad, gate_attend_grad,
                shift_feed_grad, scale_feed_grad, gate_feed_grad,
            ]
        ).astype(bf16)
        last = jnp.concatenate(
            [jnp.broadcast_to(mod_grad, (devices, 6 * D))]
            + [g.astype(bf16).reshape(devices, -1) for g in (g_bqkv, g_bout, g_bup, g_bdown)],
            axis=1,
        )
        last = spread(last, ALL)
        all_mod = last[:, : 6 * D]
        g_wmod = outer_sum(pieces, all_mod)
        device = lax.axis_index(ALL)
        g_bmod = jnp.sum(
            lax.dynamic_index_in_dim(
                all_mod.reshape(devices, devices, -1), device, 1, keepdims=False
            ).astype(f32),
            axis=0,
        )
        bias_sums = jnp.sum(last[:, 6 * D :].astype(f32), axis=0)
        at = 0
        sums = []
        for bias in (b_qkv, b_out, b_up, b_down):
            sums.append(bias_sums[at : at + bias.shape[0]])
            at += bias.shape[0]
        return (
            layer_out[None].astype(bf16), input_grad[None].astype(bf16),
            g_wqkv, sums[0], g_wout, sums[1], g_wup, sums[2], g_wdown, sums[3], g_wmod, g_bmod,
        )

    return shards


def solution(mesh):
    dp, seq = mesh.shape["dp"], mesh.shape["seq"]
    sizes = {"p": dp // 2, "c": 2, "r": seq // 2, "q": 2}
    fine = Mesh(mesh.devices.reshape(dp // 2, 2, seq // 2, 2), ALL)
    rows = P(("p", "c"), SEQ, None)
    weight, bias = P(ALL, None), P(ALL)
    pairs = (weight, bias)
    return jax.shard_map(
        make_shards(sizes),
        mesh=fine,
        in_specs=(rows, rows, P(("p", "c")), P(("p", "c"), SEQ)) + pairs * 5,
        out_specs=(rows, rows) + pairs * 5,
        check_vma=False,
    )
```

```python
import math

import jax
import jax.numpy as jnp
from jax import lax
from jax.experimental import pallas as pl
from jax.experimental.pallas import tpu as pltpu
from jax.sharding import Mesh, PartitionSpec as P

D = 1024
H = 16
HD = 64
PW = 16
EPS = 1e-06

ALL = ("p", "c", "r", "q")
SEQ = ("r", "q")
bf16 = jnp.bfloat16
SHORT = pl.CostEstimate(flops=1, bytes_accessed=1, transcendentals=0)
f32 = jnp.float32


def layer_norm(values):
    row_mean = jnp.mean(values, axis=-1, keepdims=True)
    centred = values - row_mean
    inv_std = lax.rsqrt(jnp.mean(centred * centred, axis=-1, keepdims=True) + EPS)
    return (centred * inv_std, inv_std)


def norm_back(normed, inv_std, normed_grad):
    first_mean = jnp.mean(normed_grad, axis=-1, keepdims=True)
    second_mean = jnp.mean(normed_grad * normed, axis=-1, keepdims=True)
    return inv_std * (normed_grad - first_mean - normed * second_mean)


def level_embedding(effective, width):
    half_width = width // 2
    frequency = jnp.exp(
        -math.log(10000.0) * jnp.arange(half_width).astype(f32) / half_width
    )
    angles = effective.astype(f32)[..., None] * frequency
    return jnp.concatenate([jnp.cos(angles), jnp.sin(angles)], axis=-1)


def rope_angles(frame_pos, row_pos, column_pos, head_width):
    pair_count = head_width // 2
    time_pairs = head_width // 8
    space_pairs = 3 * head_width // 16
    pair_index = jnp.arange(pair_count)
    axis_pick = jnp.where(
        pair_index < time_pairs, 0, jnp.where(pair_index < time_pairs + space_pairs, 1, 2)
    )
    local_rank = jnp.where(
        axis_pick == 0,
        pair_index,
        jnp.where(axis_pick == 1, pair_index - time_pairs, pair_index - time_pairs - space_pairs),
    )
    group_size = jnp.where(axis_pick == 0, time_pairs, space_pairs)
    frequency = jnp.exp(-math.log(10000.0) * local_rank.astype(f32) / group_size.astype(f32))
    position = jnp.where(
        axis_pick == 0,
        frame_pos[:, None],
        jnp.where(axis_pick == 1, row_pos[:, None], column_pos[:, None]),
    )
    return position.astype(f32) * frequency


def outer_sum(left, right):
    return lax.dot_general(
        left, right, (((0,), (0,)), ((), ())), preferred_element_type=f32
    )


def back_dot(grads, weight):
    return lax.dot_general(
        grads, weight, (((1,), (1,)), ((), ())), preferred_element_type=f32
    )


def nt(a, b):
    return lax.dot_general(a, b, (((1,), (1,)), ((), ())), preferred_element_type=f32)


def dot(a, b):
    return jnp.dot(a, b, preferred_element_type=f32)


def full_block(shape):
    return pl.BlockSpec(shape, lambda *_: (0,) * len(shape))


def project_kernel(
    heads, rows_ref, mod_ref, weight_ref, bias_ref, cos_ref, sin_ref,
    hidden_ref, q_ref, k_ref, kt_ref, v_ref, vt_ref,
):
    normed, _ = layer_norm(rows_ref[0].astype(f32))
    hidden = (normed * (1.0 + mod_ref[0, 1:2, :]) + mod_ref[0, 0:1, :]).astype(bf16)
    hidden_ref[...] = hidden
    made = dot(hidden, weight_ref[...]) + bias_ref[...]
    wide = heads * HD
    cosine, sine = cos_ref[...], sin_ref[...]

    def turn(values):
        half = HD // 2
        turned = jnp.concatenate([values[:, half:], values[:, :half]], axis=1)
        return values * cosine + turned * sine

    for h in range(heads):
        at = h * HD
        query = turn(made[:, at : at + HD]).astype(bf16).astype(f32)
        key = turn(made[:, wide + at : wide + at + HD])
        value = made[:, 2 * wide + at : 2 * wide + at + HD]
        q_ref[h] = (query * (1.0 / math.sqrt(HD))).astype(bf16)
        k_ref[h] = key.astype(bf16)
        kt_ref[h] = jnp.transpose(key).astype(bf16)
        v_ref[h] = value.astype(bf16)
        vt_ref[h] = jnp.transpose(value).astype(bf16)


def project(clip, frame_mod, weight, bias, cosine, sine, heads):
    frames, block, _ = clip.shape
    tokens = frames * block
    wide = heads * HD
    tall = pl.BlockSpec((heads, block, HD), lambda i: (0, i, 0))
    flat = pl.BlockSpec((heads, HD, block), lambda i: (0, 0, i))
    tall_shape = jax.ShapeDtypeStruct((heads, tokens, HD), bf16)
    flat_shape = jax.ShapeDtypeStruct((heads, HD, tokens), bf16)
    return pl.pallas_call(
        lambda *refs: project_kernel(heads, *refs),
        grid=(frames,),
        in_specs=[
            pl.BlockSpec((1, block, D), lambda i: (i, 0, 0)),
            pl.BlockSpec((1, 2, D), lambda i: (i, 0, 0)),
            full_block((D, 3 * wide)),
            full_block((1, 3 * wide)),
            pl.BlockSpec((block, HD), lambda i: (i, 0)),
            pl.BlockSpec((block, HD), lambda i: (i, 0)),
        ],
        out_specs=[pl.BlockSpec((block, D), lambda i: (i, 0)), tall, tall, flat, tall, flat],
        out_shape=[
            jax.ShapeDtypeStruct((tokens, D), bf16),
            tall_shape, tall_shape, flat_shape, tall_shape, flat_shape,
        ],
        compiler_params=pltpu.CompilerParams(vmem_limit_bytes=40 << 20),
        cost_estimate=SHORT,
    )(clip, frame_mod, weight, bias, cosine, sine)


def attend_kernel(
    block, heads, frames, q_ref, k_ref, vt_ref, ot_ref, out_ref, lse_ref, score_ref
):
    count = frames + 1

    def pair_step(first, _):
        second = frames - 1 - first

        def place(n):
            early = n <= first
            query_frame = jnp.where(early, first, second)
            key_frame = jnp.where(early, n, n - first - 1)
            return (
                early,
                pl.ds(pl.multiple_of(query_frame * block, block), block),
                pl.ds(pl.multiple_of(key_frame * block, block), block),
            )

        for h in range(heads):
            tops = []
            for n in range(count):
                _, rows, keys = place(n)
                scores = nt(k_ref[h, keys, :], q_ref[h, rows, :])
                score_ref[h, n] = scores
                tops.append(jnp.max(scores, axis=0, keepdims=True))
            low = jnp.full((1, block), -1e30, f32)
            top_a, top_b = low, low
            for n in range(count):
                early = n <= first
                top_a = jnp.maximum(top_a, jnp.where(early, tops[n], low))
                top_b = jnp.maximum(top_b, jnp.where(early, low, tops[n]))
            zero = jnp.zeros((1, block), f32)
            sum_a, sum_b = zero, zero
            acc_a = jnp.zeros((HD, block), f32)
            acc_b = acc_a
            for n in range(count):
                early, _, keys = place(n)
                weights = jnp.exp(score_ref[h, n] - jnp.where(early, top_a, top_b))
                part_sum = jnp.sum(weights, axis=0, keepdims=True)
                part = dot(vt_ref[h, :, keys], weights.astype(bf16))
                if n == 0:
                    sum_a, acc_a = part_sum, part
                elif n > (frames - 1) // 2:
                    sum_b, acc_b = sum_b + part_sum, acc_b + part
                else:
                    sum_a = sum_a + jnp.where(early, part_sum, 0.0)
                    sum_b = sum_b + jnp.where(early, 0.0, part_sum)
                    acc_a = acc_a + jnp.where(early, part, 0.0)
                    acc_b = acc_b + jnp.where(early, 0.0, part)
            for frame, top, total, acc in (
                (first, top_a, sum_a, acc_a), (second, top_b, sum_b, acc_b),
            ):
                rows = pl.ds(pl.multiple_of(frame * block, block), block)
                done = acc / total
                ot_ref[h, :, rows] = done
                out_ref[frame, :, h * HD : (h + 1) * HD] = jnp.transpose(done).astype(bf16)
                lse_ref[h, :, rows] = top + jnp.log(total)
        return 0

    lax.fori_loop(0, frames // 2, pair_step, 0)


def attend(queries, keys, values_t, block):
    heads, tokens, _ = queries.shape
    frames = tokens // block
    return pl.pallas_call(
        lambda *refs: attend_kernel(block, heads, frames, *refs),
        out_shape=[
            jax.ShapeDtypeStruct((heads, HD, tokens), f32),
            jax.ShapeDtypeStruct((frames, block, heads * HD), bf16),
            jax.ShapeDtypeStruct((heads, 1, tokens), f32),
        ],
        scratch_shapes=[pltpu.VMEM((heads, frames + 1, block, block), f32)],
        compiler_params=pltpu.CompilerParams(vmem_limit_bytes=40 << 20),
        cost_estimate=SHORT,
    )(queries, keys, values_t)


def attend_back_kernel(
    block, heads, frames, q_ref, k_ref, kt_ref, v_ref, do_ref, ot_ref, lse_ref, cos_ref, sin_ref,
    out_ref, dqt_ref, delta_ref,
):
    dqt_ref[...] = jnp.zeros_like(dqt_ref)
    wide = heads * HD
    scale = 1.0 / math.sqrt(HD)
    for i in range(frames):
        rows = slice(i * block, (i + 1) * block)
        for h in range(heads):
            grad_t = jnp.transpose(do_ref[i, :, h * HD : (h + 1) * HD].astype(f32))
            delta_ref[h, :, rows] = jnp.sum(grad_t * ot_ref[h, :, rows], axis=0, keepdims=True)

    def back(values, rows):
        half = HD // 2
        turned = jnp.concatenate([values[:, half:], values[:, :half]], axis=1)
        return (values * cos_ref[rows, :] - turned * sin_ref[rows, :]).astype(bf16)

    def pair_step(first, _):
        second = frames - 1 - first
        for h in range(heads):
            zero = jnp.zeros((block, HD), f32)
            dk_a, dv_a, dk_b, dv_b = zero, zero, zero, zero
            for n in range(frames + 1):
                early = n < frames - first
                query_frame = jnp.where(early, first + n, n - 1)
                key_frame = jnp.where(early, first, second)
                rows = pl.ds(pl.multiple_of(query_frame * block, block), block)
                keys = pl.ds(pl.multiple_of(key_frame * block, block), block)
                query = q_ref[h, rows, :]
                grad = do_ref[query_frame, :, h * HD : (h + 1) * HD]
                probs = jnp.exp(nt(k_ref[h, keys, :], query) - lse_ref[h, :, rows])
                prob_grad = nt(v_ref[h, keys, :], grad)
                score_grad = (probs * (prob_grad - delta_ref[h, :, rows])).astype(bf16)
                dv = dot(probs.astype(bf16), grad)
                dk = dot(score_grad, query)
                dqt_ref[h, :, rows] += dot(kt_ref[h, :, keys], score_grad)
                if n < frames - (frames - 1) // 2:
                    dk_a, dv_a = dk_a + dk, dv_a + dv
                elif n == frames:
                    dk_b, dv_b = dk_b + dk, dv_b + dv
                else:
                    dk_a = dk_a + jnp.where(early, dk, 0.0)
                    dv_a = dv_a + jnp.where(early, dv, 0.0)
                    dk_b = dk_b + jnp.where(early, 0.0, dk)
                    dv_b = dv_b + jnp.where(early, 0.0, dv)
            for frame, dk, dv in ((first, dk_a, dv_a), (second, dk_b, dv_b)):
                rows = pl.ds(pl.multiple_of(frame * block, block), block)
                at = wide + h * HD
                out_ref[frame, :, at : at + HD] = back(dk, rows)
                out_ref[frame, :, wide + at : wide + at + HD] = dv.astype(bf16)
        return 0

    lax.fori_loop(0, frames // 2, pair_step, 0)
    for i in range(frames):
        rows = slice(i * block, (i + 1) * block)
        for h in range(heads):
            out_ref[i, :, h * HD : (h + 1) * HD] = back(
                jnp.transpose(dqt_ref[h, :, rows]) * scale, rows
            )


def attend_back(queries, keys, keys_t, values, grad, out_t, lse, cosine, sine, block):
    heads, tokens, _ = queries.shape
    frames = tokens // block
    return pl.pallas_call(
        lambda *refs: attend_back_kernel(block, heads, frames, *refs),
        out_shape=jax.ShapeDtypeStruct((frames, block, 3 * heads * HD), bf16),
        scratch_shapes=[
            pltpu.VMEM((heads, HD, tokens), f32),
            pltpu.VMEM((heads, 1, tokens), f32),
        ],
        compiler_params=pltpu.CompilerParams(vmem_limit_bytes=48 << 20),
        cost_estimate=SHORT,
    )(queries, keys, keys_t, values, grad, out_t, lse, cosine, sine)


def middle_kernel(
    parts, tiles, att_ref, in_ref, cot_ref, mod_ref, live_ref, out_bias_ref, down_bias_ref,
    up_bias_ref, w_out_ref, w_up_ref, w_down_ref,
    layer_ref, grad_ref, act_ref, up_grad_ref, two_grad_ref, half_ref,
    att_grad_ref, stat_ref, g_bup_ref,
    att_all, branch_ref, middle_ref, normed_ref, inv_ref, hidden_ref, down_acc, back_acc,
):
    tile = pl.program_id(0)
    gate_a, shift_f, scale_f, gate_f = (mod_ref[i : i + 1, :] for i in (2, 3, 4, 5))
    groups, _, wide = att_ref.shape
    span = D // (2 * parts)

    def flat(ref):
        last = ref.shape[-1]
        return jnp.concatenate(
            [ref[:, p].reshape(-1, last) for p in range(ref.shape[1])], axis=0
        )

    def halves(start, values):
        for p in range(parts):
            for c in range(2):
                at = (2 * p + c) * span
                to = start + p * span
                half_ref[c, :, to : to + span] = values[:, at : at + span]

    @pl.when(tile == 0)
    def _():
        for g in range(groups):
            att_all[:, g * wide : (g + 1) * wide] = att_ref[g]
        attended = att_all[...]
        halves(D // 2, attended)
        branch = dot(attended, flat(w_out_ref)) + out_bias_ref[...]
        branch_ref[...] = branch
        middle = in_ref[...].astype(f32) + gate_a * branch
        middle_ref[...] = middle
        normed, inv_std = layer_norm(middle)
        normed_ref[...] = normed
        inv_ref[...] = inv_std
        hidden = (normed * (1.0 + scale_f) + shift_f).astype(bf16)
        hidden_ref[...] = hidden
        halves(0, hidden)
        two_grad_ref[0] = (cot_ref[...].astype(f32) * live_ref[...] * gate_f).astype(bf16)

    hidden = hidden_ref[...]
    down_grad = two_grad_ref[0]
    w_up, w_down = flat(w_up_ref), flat(w_down_ref)
    u = dot(hidden, w_up) + up_bias_ref[...]
    scale = math.sqrt(2.0 / math.pi)
    square = u * u
    bend = jnp.tanh(scale * (u + 0.044715 * (u * square)))
    rise = 0.5 * (1.0 + bend)
    slope = rise + (0.5 * scale) * u * (1.0 - bend * bend) * (1.0 + (3.0 * 0.044715) * square)
    act = (u * rise).astype(bf16)
    act_ref[0] = act
    down_part = dot(act, w_down)
    up_grad = (nt(down_grad, w_down) * slope).astype(bf16)
    up_grad_ref[...] = up_grad
    g_bup_ref[...] = jnp.sum(up_grad.astype(f32), axis=0, keepdims=True)
    back_part = nt(up_grad, w_up)

    @pl.when(tile == 0)
    def _():
        down_acc[...] = down_part
        back_acc[...] = back_part

    @pl.when(tile > 0)
    def _():
        down_acc[...] += down_part
        back_acc[...] += back_part

    @pl.when(tile == tiles - 1)
    def _():
        def put(at, values):
            stat_ref[at : at + 1, :] = jnp.sum(values, axis=0, keepdims=True)

        out_grad = cot_ref[...].astype(f32) * live_ref[...]
        down_rows = down_acc[...] + down_bias_ref[...]
        layer_ref[...] = (middle_ref[...] + gate_f * down_rows).astype(bf16)
        put(3, out_grad * down_rows)
        put(4, down_grad.astype(f32))
        hidden_grad = back_acc[...]
        normed = normed_ref[...]
        put(1, hidden_grad)
        put(2, hidden_grad * normed)
        middle_grad = out_grad + norm_back(normed, inv_ref[...], hidden_grad * (1.0 + scale_f))
        grad_ref[...] = middle_grad
        put(0, middle_grad * branch_ref[...])
        branch_grad = (middle_grad * gate_a).astype(bf16)
        two_grad_ref[1] = branch_grad
        put(5, branch_grad.astype(f32))
        put(6, jnp.zeros_like(out_grad))
        put(7, jnp.zeros_like(out_grad))
        att_grad = nt(branch_grad, flat(w_out_ref)).astype(bf16)
        for g in range(groups):
            att_grad_ref[g] = att_grad[:, g * wide : (g + 1) * wide]


def middle(attended, rows, cot, mod, live, biases, stack, parts):
    groups, patches, wide = attended.shape
    hidden_units = biases[2].shape[1]
    devices = stack.shape[0] * parts
    down_rows, up_rows = hidden_units // devices, D // devices
    first_up, first_out = down_rows // up_rows, (down_rows + up_rows * (hidden_units // D)) // up_rows
    span = hidden_units // (2 * parts)
    width = min(512, span)
    tiles = hidden_units // width
    tiles_part = tiles // parts
    per_span = span // width

    def half_at(t):
        block = t // per_span
        return (block % 2, 0, (block // 2) * per_span + t % per_span)

    token_shape = (patches, D)

    def shape(dims, dtype):
        return jax.ShapeDtypeStruct(dims, dtype)

    return pl.pallas_call(
        lambda *refs: middle_kernel(parts, tiles, *refs),
        grid=(tiles,),
        in_specs=[
            full_block(attended.shape), full_block(token_shape), full_block(token_shape),
            full_block((6, D)), full_block((1, 1)), full_block((1, D)), full_block((1, D)),
            pl.BlockSpec((1, width), lambda t: (0, t)),
            pl.BlockSpec((devices // parts, parts, up_rows, D), lambda t: (0, 0, first_out, 0)),
            pl.BlockSpec(
                (devices // parts, parts, up_rows, width),
                lambda t: (0, 0, first_up + t * width // D, t % (D // width)),
            ),
            pl.BlockSpec(
                (width // down_rows, 1, down_rows, D),
                lambda t: (t % tiles_part, t // tiles_part, 0, 0),
            ),
        ],
        out_specs=[
            full_block(token_shape), full_block(token_shape),
            pl.BlockSpec((1, patches, width), half_at),
            pl.BlockSpec((patches, width), lambda t: (0, t)),
            full_block((2,) + token_shape), full_block((2,) + token_shape),
            full_block(attended.shape), full_block((8, D)),
            pl.BlockSpec((1, width), lambda t: (0, t)),
        ],
        out_shape=[
            shape(token_shape, bf16), shape(token_shape, f32),
            shape((2, patches, hidden_units // 2), bf16), shape((patches, hidden_units), bf16),
            shape((2,) + token_shape, bf16), shape((2,) + token_shape, bf16),
            shape(attended.shape, bf16), shape((8, D), f32),
            shape((1, hidden_units), f32),
        ],
        scratch_shapes=[
            pltpu.VMEM(token_shape, bf16), pltpu.VMEM(token_shape, f32),
            pltpu.VMEM(token_shape, f32), pltpu.VMEM(token_shape, f32),
            pltpu.VMEM((patches, 1), f32), pltpu.VMEM(token_shape, bf16),
            pltpu.VMEM(token_shape, f32), pltpu.VMEM(token_shape, f32),
        ],
        compiler_params=pltpu.CompilerParams(vmem_limit_bytes=56 << 20),
        cost_estimate=SHORT,
    )(attended, rows, cot, mod, live, *biases, stack, stack, stack)


def swap(values, axis):
    return lax.ppermute(values, axis, [(0, 1), (1, 0)])


def shifts(values, axis, size):
    me = lax.axis_index(axis)
    found = [(me, values)]
    for shift in range(1, size):
        pairs = [(i, (i + shift) % size) for i in range(size)]
        found.append(((me + size - shift) % size, lax.ppermute(values, axis, pairs)))
    return found


def line_gather(values, axis, size):
    whole = jnp.zeros((size,) + values.shape, values.dtype)
    for place, part in shifts(values, axis, size):
        whole = lax.dynamic_update_index_in_dim(whole, part, place, 0)
    return whole


def line_parts(parts, axis, size):
    me = lax.axis_index(axis)
    kept = lax.dynamic_index_in_dim(parts, me, 0, keepdims=False)
    theirs = [
        lax.dynamic_index_in_dim(parts, (me + shift) % size, 0, keepdims=False)
        for shift in range(1, size)
    ]
    return kept, theirs


def line_move(theirs, axis, size):
    return [
        lax.ppermute(part, axis, [(i, (i + shift) % size) for i in range(size)])
        for shift, part in enumerate(theirs, 1)
    ]


def line_send(parts, axis, size):
    kept, theirs = line_parts(parts, axis, size)
    return kept, line_move(theirs, axis, size)


def add_up(kept, got):
    total = kept.astype(f32)
    for part in got:
        total = total + part.astype(f32)
    return total


def after(values, earlier):
    return lax.optimization_barrier((values, earlier))[0]


def make_shards(sizes):
    seq = sizes["r"] * sizes["q"]
    dp = sizes["p"] * sizes["c"]
    devices = seq * dp
    heads = H // seq
    wide = heads * HD

    def spread(values, axes):
        return lax.all_to_all(values, axes, 0, 0, tiled=True)

    def shards(
        inputs, cotangent, context, levels, w_qkv, b_qkv, w_out, b_out, w_up, b_up,
        w_down, b_down, w_mod, b_mod,
    ):
        own_frame = lax.axis_index(SEQ)
        core = lax.axis_index("c")
        patches = inputs.shape[1]
        tokens = seq * patches
        own_rows = w_mod.shape[0]

        effective = jnp.where(own_frame < context, 0, levels[:, 0])
        condition = jax.nn.silu(level_embedding(effective, D)).astype(bf16)
        biases = jnp.concatenate([b_qkv, b_out, b_up, b_down, b_mod])
        first = jnp.concatenate(
            [
                condition.reshape(devices, own_rows),
                jnp.broadcast_to(biases, (devices, biases.shape[0])),
            ],
            axis=1,
        )
        first = spread(first, ALL)
        pieces = first[:, :own_rows]
        at = own_rows
        full = []
        for bias in (b_qkv, b_out, b_up, b_down, b_mod):
            size = bias.shape[0]
            full.append(first[:, at : at + size].reshape(-1).astype(f32))
            at += size
        qkv_bias, out_bias, up_bias, down_bias, mod_bias = full
        mod_parts = jnp.dot(pieces, w_mod, preferred_element_type=f32).astype(bf16)
        modulation = jnp.sum(spread(mod_parts, ALL).astype(f32), axis=0) + mod_bias
        scale_attend = modulation[None, D : 2 * D]
        frame_mod = spread(jnp.broadcast_to(modulation[None, : 2 * D], (seq, 2 * D)), SEQ)

        own_qkv = jnp.transpose(w_qkv.reshape(own_rows, 3, seq, wide), (2, 0, 1, 3))
        own_qkv = spread(own_qkv.reshape(seq, own_rows, 3 * wide), SEQ)
        own_qkv = line_gather(line_gather(own_qkv, "c", sizes["c"]), "p", sizes["p"])
        own_qkv = own_qkv.reshape(D, 3 * wide)

        rows = inputs[0]
        clip = lax.all_gather(rows, SEQ, axis=0, tiled=False)

        def whole(weight):
            return lax.all_gather(weight, ALL, axis=0, tiled=True)

        stack = jnp.concatenate(
            [w_down] + [w_up[:, at : at + D] for at in range(0, w_up.shape[1], D)] + [w_out]
        )
        stack = line_gather(stack, "p", sizes["p"])
        stack = lax.all_gather(stack, ("c", "r", "q"), axis=0, tiled=False)
        qkv_weight = whole(after(w_qkv, stack))

        own_bias = lax.dynamic_index_in_dim(
            qkv_bias.reshape(3, seq, wide), own_frame, 1, keepdims=False
        ).reshape(1, 3 * wide)
        token = jnp.arange(tokens)
        patch = token % patches
        angles = rope_angles(token // patches, patch // PW, patch % PW, HD)
        cosine, sine = jnp.cos(angles), jnp.sin(angles)
        cosine = jnp.concatenate([cosine, cosine], axis=-1)
        sine = jnp.concatenate([-sine, sine], axis=-1)
        hidden_all, queries, keys, keys_t, values, values_t = project(
            clip, frame_mod.reshape(seq, 2, D), own_qkv, own_bias, cosine, sine, heads
        )
        out_t, attended, lse = attend(queries, keys, values_t, patches)

        attended = spread(attended, SEQ)
        live = (own_frame >= context).astype(f32)[:, None]
        (
            layer_out, middle_grad, activated, up_grad, two_grads, left_halves, attended_grad,
            stats, g_bup,
        ) = middle(
            attended, rows, cotangent[0], modulation.reshape(6, D), live,
            (out_bias[None], down_bias[None], up_bias[None]), stack, sizes["p"],
        )
        gate_attend_grad, shift_feed_grad, scale_feed_grad, gate_feed_grad = (
            stats[i] for i in range(4)
        )
        g_bdown, g_bout = stats[4], stats[5]
        attended_grad = spread(attended_grad, SEQ)

        def both_cores(values):
            mine = lax.dynamic_index_in_dim(values, core, 0, keepdims=False)
            theirs = lax.dynamic_index_in_dim(values, 1 - core, 0, keepdims=False)
            return jnp.concatenate([mine, swap(theirs, "c")])

        two_got = swap(two_grads, "c")
        right = jnp.concatenate([two_grads, two_got], axis=1)
        activated = both_cores(activated)
        left_halves = both_cores(left_halves)
        up_grad = jnp.concatenate([up_grad, swap(up_grad, "c")])

        def by_chip(total):
            return total.astype(bf16).reshape(
                sizes["p"], sizes["r"], sizes["q"], -1, total.shape[1]
            )

        g_down = by_chip(outer_sum(activated, right[0]))
        g_up = by_chip(outer_sum(left_halves[:, : D // 2], up_grad))
        g_out = by_chip(outer_sum(left_halves[:, D // 2 :], right[1]))

        def columns(values, part):
            half = values.shape[-1] // 2
            return values[..., :half] if part == 0 else values[..., half:]

        groups = []
        for arrays in ((g_down,), (g_up, g_out)):
            one = [jnp.moveaxis(columns(values, 0), 2, 0) for values in arrays]
            two = [jnp.moveaxis(columns(values, 1), 2, 1) for values in arrays]
            one, two = (jnp.concatenate(parts, axis=-1) for parts in (one, two))
            groups.append((line_parts(one, "q", sizes["q"]), line_parts(two, "p", sizes["p"])))

        attended_grad = after(attended_grad, groups)
        groups = [
            tuple(
                (kept, line_move(theirs, axis, sizes[axis]))
                for (kept, theirs), axis in zip(group, ("q", "p"))
            )
            for group in groups
        ]
        dqkv = attend_back(
            queries, keys, keys_t, values, attended_grad, out_t, lse, cosine, sine, patches,
        ).reshape(tokens, 3 * wide)
        qkv_got = spread(dqkv.reshape(seq, patches, 3 * wide), SEQ)
        g_own = outer_sum(hidden_all, dqkv).astype(bf16).reshape(
            sizes["p"], sizes["c"], seq, own_rows, 3 * wide
        )
        own_send = line_send(jnp.moveaxis(g_own, 1, 0), "c", sizes["c"])
        seconds = []
        for one, two in groups:
            one, two = (add_up(kept, after(got, dqkv)).astype(bf16) for kept, got in (one, two))
            seconds.append((line_send(one, "p", sizes["p"]), line_send(two, "q", sizes["q"])))
        own_sum = add_up(*own_send).astype(bf16)
        own_sum = add_up(*line_send(own_sum, "p", sizes["p"])).astype(bf16)
        own_sum = own_sum.reshape(sizes["r"], sizes["q"], own_rows, 3 * wide)
        own_kept, own_got = line_send(jnp.moveaxis(own_sum, 1, 0), "q", sizes["q"])
        qkv_got, seconds, own_got = lax.optimization_barrier((qkv_got, seconds, own_got))
        first_q = lax.axis_index("q") == 0
        own_got = own_got[0]
        own_pair = jnp.concatenate(
            [jnp.where(first_q, own_kept, own_got), jnp.where(first_q, own_got, own_kept)],
            axis=-1,
        )
        thirds = []
        for (one, two), more in zip(seconds, ((), (own_pair,))):
            both = jnp.concatenate([add_up(*one), add_up(*two)], axis=-1).astype(bf16)
            thirds.append(line_send(jnp.concatenate((both,) + more, axis=-1), "r", sizes["r"]))

        qkv_grad = jnp.transpose(
            qkv_got.reshape(seq, patches, 3, wide), (1, 2, 0, 3)
        ).reshape(patches, 3 * D)
        g_bqkv = jnp.sum(qkv_grad.astype(f32), axis=0)
        start_rows = rows.astype(f32)
        hidden_grad = back_dot(qkv_grad, qkv_weight)
        normed, inv_std = layer_norm(start_rows)
        scale_attend_grad = jnp.sum(hidden_grad * normed, axis=0)
        shift_attend_grad = jnp.sum(hidden_grad, axis=0)
        input_grad = middle_grad + norm_back(
            normed, inv_std, hidden_grad * (1.0 + scale_attend)
        )

        mod_grad = jnp.concatenate(
            [
                shift_attend_grad, scale_attend_grad, gate_attend_grad,
                shift_feed_grad, scale_feed_grad, gate_feed_grad,
            ]
        ).astype(bf16)
        last = jnp.concatenate(
            [jnp.broadcast_to(mod_grad, (devices, 6 * D))]
            + [g.astype(bf16).reshape(devices, -1) for g in (g_bqkv, g_bout, g_bup, g_bdown)],
            axis=1,
        )
        last_got = spread(last, ALL)
        all_mod = last_got[:, : 6 * D]
        g_wmod = outer_sum(pieces, all_mod)
        device = lax.axis_index(ALL)
        g_bmod = jnp.sum(
            lax.dynamic_index_in_dim(
                all_mod.reshape(devices, devices, -1), device, 1, keepdims=False
            ).astype(f32),
            axis=0,
        )
        bias_sums = jnp.sum(last_got[:, 6 * D :].astype(f32), axis=0)
        at = 0
        sums = []
        for bias in (b_qkv, b_out, b_up, b_down):
            sums.append(bias_sums[at : at + bias.shape[0]])
            at += bias.shape[0]
        thirds = [(kept, after(got, last)) for kept, got in thirds]
        kept, got = thirds[1]
        own_width = 6 * wide
        place = lax.axis_index("r")
        g_wqkv = jnp.zeros((sizes["r"], own_rows, own_width), bf16)
        for shift, part in enumerate([kept] + list(got)):
            g_wqkv = lax.dynamic_update_index_in_dim(
                g_wqkv, part[:, -own_width:], (place - shift) % sizes["r"], 0
            )
        g_wqkv = jnp.transpose(
            g_wqkv.reshape(sizes["r"], own_rows, 2, 3, wide), (1, 3, 0, 2, 4)
        ).reshape(own_rows, 3 * D).astype(f32)
        g_wdown = add_up(*thirds[0])
        second_sum = add_up(kept[:, :-own_width], [part[:, :-own_width] for part in got])
        half_up, half = w_up.shape[1] // 2, second_sum.shape[1] // 2
        g_wup = jnp.concatenate([second_sum[:, :half_up], second_sum[:, half : half + half_up]], axis=1)
        g_wout = jnp.concatenate([second_sum[:, half_up:half], second_sum[:, half + half_up :]], axis=1)
        return (
            layer_out[None].astype(bf16), input_grad[None].astype(bf16),
            g_wqkv, sums[0], g_wout, sums[1], g_wup, sums[2], g_wdown, sums[3], g_wmod, g_bmod,
        )

    return shards


def solution(mesh):
    dp, seq = mesh.shape["dp"], mesh.shape["seq"]
    sizes = {"p": dp // 2, "c": 2, "r": seq // 2, "q": 2}
    fine = Mesh(mesh.devices.reshape(dp // 2, 2, seq // 2, 2), ALL)
    rows = P(("p", "c"), SEQ, None)
    weight, bias = P(ALL, None), P(ALL)
    pairs = (weight, bias)
    return jax.shard_map(
        make_shards(sizes),
        mesh=fine,
        in_specs=(rows, rows, P(("p", "c")), P(("p", "c"), SEQ)) + pairs * 5,
        out_specs=(rows, rows) + pairs * 5,
        check_vma=False,
    )
```

```python
import math

import jax
import jax.numpy as jnp
from jax import lax
from jax.experimental import pallas as pl
from jax.experimental.pallas import tpu as pltpu
from jax.sharding import Mesh, PartitionSpec as P

D = 1024
H = 16
HD = 64
PW = 16
EPS = 1e-06

ALL = ("p", "c", "r", "q")
SEQ = ("r", "q")
bf16 = jnp.bfloat16
SHORT = pl.CostEstimate(flops=1, bytes_accessed=1, transcendentals=0)
f32 = jnp.float32


def layer_norm(values):
    row_mean = jnp.mean(values, axis=-1, keepdims=True)
    centred = values - row_mean
    inv_std = lax.rsqrt(jnp.mean(centred * centred, axis=-1, keepdims=True) + EPS)
    return (centred * inv_std, inv_std)


def norm_back(normed, inv_std, normed_grad):
    first_mean = jnp.mean(normed_grad, axis=-1, keepdims=True)
    second_mean = jnp.mean(normed_grad * normed, axis=-1, keepdims=True)
    return inv_std * (normed_grad - first_mean - normed * second_mean)


def level_embedding(effective, width):
    half_width = width // 2
    frequency = jnp.exp(
        -math.log(10000.0) * jnp.arange(half_width).astype(f32) / half_width
    )
    angles = effective.astype(f32)[..., None] * frequency
    return jnp.concatenate([jnp.cos(angles), jnp.sin(angles)], axis=-1)


def rope_angles(frame_pos, row_pos, column_pos, head_width):
    pair_count = head_width // 2
    time_pairs = head_width // 8
    space_pairs = 3 * head_width // 16
    pair_index = jnp.arange(pair_count)
    axis_pick = jnp.where(
        pair_index < time_pairs, 0, jnp.where(pair_index < time_pairs + space_pairs, 1, 2)
    )
    local_rank = jnp.where(
        axis_pick == 0,
        pair_index,
        jnp.where(axis_pick == 1, pair_index - time_pairs, pair_index - time_pairs - space_pairs),
    )
    group_size = jnp.where(axis_pick == 0, time_pairs, space_pairs)
    frequency = jnp.exp(-math.log(10000.0) * local_rank.astype(f32) / group_size.astype(f32))
    position = jnp.where(
        axis_pick == 0,
        frame_pos[:, None],
        jnp.where(axis_pick == 1, row_pos[:, None], column_pos[:, None]),
    )
    return position.astype(f32) * frequency


def outer_sum(left, right):
    return lax.dot_general(
        left, right, (((0,), (0,)), ((), ())), preferred_element_type=f32
    )


def back_dot(grads, weight):
    return lax.dot_general(
        grads, weight, (((1,), (1,)), ((), ())), preferred_element_type=f32
    )


def nt(a, b):
    return lax.dot_general(a, b, (((1,), (1,)), ((), ())), preferred_element_type=f32)


def dot(a, b):
    return jnp.dot(a, b, preferred_element_type=f32)


def full_block(shape):
    return pl.BlockSpec(shape, lambda *_: (0,) * len(shape))


def project_kernel(
    heads, rows_ref, mod_ref, weight_ref, bias_ref, cos_ref, sin_ref,
    hidden_ref, q_ref, k_ref, kt_ref, v_ref, vt_ref,
):
    normed, _ = layer_norm(rows_ref[0].astype(f32))
    hidden = (normed * (1.0 + mod_ref[0, 1:2, :]) + mod_ref[0, 0:1, :]).astype(bf16)
    hidden_ref[...] = hidden
    made = dot(hidden, weight_ref[...]) + bias_ref[...]
    wide = heads * HD
    cosine, sine = cos_ref[...], sin_ref[...]

    def turn(values):
        half = HD // 2
        turned = jnp.concatenate([values[:, half:], values[:, :half]], axis=1)
        return values * cosine + turned * sine

    for h in range(heads):
        at = h * HD
        query = turn(made[:, at : at + HD]).astype(bf16).astype(f32)
        key = turn(made[:, wide + at : wide + at + HD])
        value = made[:, 2 * wide + at : 2 * wide + at + HD]
        q_ref[h] = (query * (1.0 / math.sqrt(HD))).astype(bf16)
        k_ref[h] = key.astype(bf16)
        kt_ref[h] = jnp.transpose(key).astype(bf16)
        v_ref[h] = value.astype(bf16)
        vt_ref[h] = jnp.transpose(value).astype(bf16)


def project(clip, frame_mod, weight, bias, cosine, sine, heads):
    frames, block, _ = clip.shape
    tokens = frames * block
    wide = heads * HD
    tall = pl.BlockSpec((heads, block, HD), lambda i: (0, i, 0))
    flat = pl.BlockSpec((heads, HD, block), lambda i: (0, 0, i))
    tall_shape = jax.ShapeDtypeStruct((heads, tokens, HD), bf16)
    flat_shape = jax.ShapeDtypeStruct((heads, HD, tokens), bf16)
    return pl.pallas_call(
        lambda *refs: project_kernel(heads, *refs),
        grid=(frames,),
        in_specs=[
            pl.BlockSpec((1, block, D), lambda i: (i, 0, 0)),
            pl.BlockSpec((1, 2, D), lambda i: (i, 0, 0)),
            full_block((D, 3 * wide)),
            full_block((1, 3 * wide)),
            pl.BlockSpec((block, HD), lambda i: (i, 0)),
            pl.BlockSpec((block, HD), lambda i: (i, 0)),
        ],
        out_specs=[pl.BlockSpec((block, D), lambda i: (i, 0)), tall, tall, flat, tall, flat],
        out_shape=[
            jax.ShapeDtypeStruct((tokens, D), bf16),
            tall_shape, tall_shape, flat_shape, tall_shape, flat_shape,
        ],
        compiler_params=pltpu.CompilerParams(vmem_limit_bytes=40 << 20),
        cost_estimate=SHORT,
    )(clip, frame_mod, weight, bias, cosine, sine)


def attend_kernel(
    block, heads, frames, q_ref, k_ref, vt_ref, ot_ref, out_ref, lse_ref, score_ref
):
    count = frames + 1

    def pair_step(first, _):
        second = frames - 1 - first

        def place(n):
            early = n <= first
            query_frame = jnp.where(early, first, second)
            key_frame = jnp.where(early, n, n - first - 1)
            return (
                early,
                pl.ds(pl.multiple_of(query_frame * block, block), block),
                pl.ds(pl.multiple_of(key_frame * block, block), block),
            )

        for h in range(heads):
            tops = []
            for n in range(count):
                _, rows, keys = place(n)
                scores = nt(k_ref[h, keys, :], q_ref[h, rows, :])
                score_ref[h, n] = scores
                tops.append(jnp.max(scores, axis=0, keepdims=True))
            low = jnp.full((1, block), -1e30, f32)
            top_a, top_b = low, low
            for n in range(count):
                early = n <= first
                top_a = jnp.maximum(top_a, jnp.where(early, tops[n], low))
                top_b = jnp.maximum(top_b, jnp.where(early, low, tops[n]))
            zero = jnp.zeros((1, block), f32)
            sum_a, sum_b = zero, zero
            acc_a = jnp.zeros((HD, block), f32)
            acc_b = acc_a
            for n in range(count):
                early, _, keys = place(n)
                weights = jnp.exp(score_ref[h, n] - jnp.where(early, top_a, top_b))
                part_sum = jnp.sum(weights, axis=0, keepdims=True)
                part = dot(vt_ref[h, :, keys], weights.astype(bf16))
                if n == 0:
                    sum_a, acc_a = part_sum, part
                elif n > (frames - 1) // 2:
                    sum_b, acc_b = sum_b + part_sum, acc_b + part
                else:
                    sum_a = sum_a + jnp.where(early, part_sum, 0.0)
                    sum_b = sum_b + jnp.where(early, 0.0, part_sum)
                    acc_a = acc_a + jnp.where(early, part, 0.0)
                    acc_b = acc_b + jnp.where(early, 0.0, part)
            for frame, top, total, acc in (
                (first, top_a, sum_a, acc_a), (second, top_b, sum_b, acc_b),
            ):
                rows = pl.ds(pl.multiple_of(frame * block, block), block)
                done = acc / total
                ot_ref[h, :, rows] = done
                out_ref[frame, :, h * HD : (h + 1) * HD] = jnp.transpose(done).astype(bf16)
                lse_ref[h, :, rows] = top + jnp.log(total)
        return 0

    lax.fori_loop(0, frames // 2, pair_step, 0)


def attend(queries, keys, values_t, block):
    heads, tokens, _ = queries.shape
    frames = tokens // block
    return pl.pallas_call(
        lambda *refs: attend_kernel(block, heads, frames, *refs),
        out_shape=[
            jax.ShapeDtypeStruct((heads, HD, tokens), f32),
            jax.ShapeDtypeStruct((frames, block, heads * HD), bf16),
            jax.ShapeDtypeStruct((heads, 1, tokens), f32),
        ],
        scratch_shapes=[pltpu.VMEM((heads, frames + 1, block, block), f32)],
        compiler_params=pltpu.CompilerParams(vmem_limit_bytes=40 << 20),
        cost_estimate=SHORT,
    )(queries, keys, values_t)


def attend_back_kernel(
    block, heads, frames, _, q_ref, k_ref, kt_ref, v_ref, do_ref, ot_ref, lse_ref, cos_ref, sin_ref,
    out_ref, dqt_ref, delta_ref,
):
    dqt_ref[...] = jnp.zeros_like(dqt_ref)
    wide = heads * HD
    scale = 1.0 / math.sqrt(HD)
    for i in range(frames):
        rows = slice(i * block, (i + 1) * block)
        for h in range(heads):
            grad_t = jnp.transpose(do_ref[i, :, h * HD : (h + 1) * HD].astype(f32))
            delta_ref[h, :, rows] = jnp.sum(grad_t * ot_ref[h, :, rows], axis=0, keepdims=True)

    def back(values, rows):
        half = HD // 2
        turned = jnp.concatenate([values[:, half:], values[:, :half]], axis=1)
        return (values * cos_ref[rows, :] - turned * sin_ref[rows, :]).astype(bf16)

    def pair_step(first, _):
        second = frames - 1 - first
        for h in range(heads):
            zero = jnp.zeros((block, HD), f32)
            dk_a, dv_a, dk_b, dv_b = zero, zero, zero, zero
            for n in range(frames + 1):
                early = n < frames - first
                query_frame = jnp.where(early, first + n, n - 1)
                key_frame = jnp.where(early, first, second)
                rows = pl.ds(pl.multiple_of(query_frame * block, block), block)
                keys = pl.ds(pl.multiple_of(key_frame * block, block), block)
                query = q_ref[h, rows, :]
                grad = do_ref[query_frame, :, h * HD : (h + 1) * HD]
                probs = jnp.exp(nt(k_ref[h, keys, :], query) - lse_ref[h, :, rows])
                prob_grad = nt(v_ref[h, keys, :], grad)
                score_grad = (probs * (prob_grad - delta_ref[h, :, rows])).astype(bf16)
                dv = dot(probs.astype(bf16), grad)
                dk = dot(score_grad, query)
                dqt_ref[h, :, rows] += dot(kt_ref[h, :, keys], score_grad)
                if n < frames - (frames - 1) // 2:
                    dk_a, dv_a = dk_a + dk, dv_a + dv
                elif n == frames:
                    dk_b, dv_b = dk_b + dk, dv_b + dv
                else:
                    dk_a = dk_a + jnp.where(early, dk, 0.0)
                    dv_a = dv_a + jnp.where(early, dv, 0.0)
                    dk_b = dk_b + jnp.where(early, 0.0, dk)
                    dv_b = dv_b + jnp.where(early, 0.0, dv)
            for frame, dk, dv in ((first, dk_a, dv_a), (second, dk_b, dv_b)):
                rows = pl.ds(pl.multiple_of(frame * block, block), block)
                at = wide + h * HD
                out_ref[frame, :, at : at + HD] = back(dk, rows)
                out_ref[frame, :, wide + at : wide + at + HD] = dv.astype(bf16)
        return 0

    lax.fori_loop(0, frames // 2, pair_step, 0)
    for i in range(frames):
        rows = slice(i * block, (i + 1) * block)
        for h in range(heads):
            out_ref[i, :, h * HD : (h + 1) * HD] = back(
                jnp.transpose(dqt_ref[h, :, rows]) * scale, rows
            )


def attend_back(order, queries, keys, keys_t, values, grad, out_t, lse, cosine, sine, block):
    heads, tokens, _ = queries.shape
    frames = tokens // block
    return pl.pallas_call(
        lambda *refs: attend_back_kernel(block, heads, frames, *refs),
        out_shape=jax.ShapeDtypeStruct((frames, block, 3 * heads * HD), bf16),
        scratch_shapes=[
            pltpu.VMEM((heads, HD, tokens), f32),
            pltpu.VMEM((heads, 1, tokens), f32),
        ],
        compiler_params=pltpu.CompilerParams(vmem_limit_bytes=48 << 20),
        cost_estimate=SHORT,
    )(order.reshape(1, 1), queries, keys, keys_t, values, grad, out_t, lse, cosine, sine)


def middle_kernel(
    parts, tiles, att_ref, in_ref, cot_ref, mod_ref, live_ref, out_bias_ref, down_bias_ref,
    up_bias_ref, w_out_ref, w_up_ref, w_down_ref,
    layer_ref, grad_ref, act_ref, up_grad_ref, two_grad_ref, half_ref,
    att_grad_ref, stat_ref, g_bup_ref,
    att_all, branch_ref, middle_ref, normed_ref, inv_ref, hidden_ref, down_acc, back_acc,
):
    tile = pl.program_id(0)
    gate_a, shift_f, scale_f, gate_f = (mod_ref[i : i + 1, :] for i in (2, 3, 4, 5))
    groups, _, wide = att_ref.shape
    span = D // (2 * parts)

    def flat(ref):
        last = ref.shape[-1]
        return jnp.concatenate(
            [ref[:, p].reshape(-1, last) for p in range(ref.shape[1])], axis=0
        )

    def halves(start, values):
        for p in range(parts):
            for c in range(2):
                at = (2 * p + c) * span
                to = start + p * span
                half_ref[c, :, to : to + span] = values[:, at : at + span]

    @pl.when(tile == 0)
    def _():
        for g in range(groups):
            att_all[:, g * wide : (g + 1) * wide] = att_ref[g]
        attended = att_all[...]
        halves(D // 2, attended)
        branch = dot(attended, flat(w_out_ref)) + out_bias_ref[...]
        branch_ref[...] = branch
        middle = in_ref[...].astype(f32) + gate_a * branch
        middle_ref[...] = middle
        normed, inv_std = layer_norm(middle)
        normed_ref[...] = normed
        inv_ref[...] = inv_std
        hidden = (normed * (1.0 + scale_f) + shift_f).astype(bf16)
        hidden_ref[...] = hidden
        halves(0, hidden)
        two_grad_ref[0] = (cot_ref[...].astype(f32) * live_ref[...] * gate_f).astype(bf16)

    hidden = hidden_ref[...]
    down_grad = two_grad_ref[0]
    w_up, w_down = flat(w_up_ref), flat(w_down_ref)
    u = dot(hidden, w_up) + up_bias_ref[...]
    scale = math.sqrt(2.0 / math.pi)
    square = u * u
    bend = jnp.tanh(scale * (u + 0.044715 * (u * square)))
    rise = 0.5 * (1.0 + bend)
    slope = rise + (0.5 * scale) * u * (1.0 - bend * bend) * (1.0 + (3.0 * 0.044715) * square)
    act = (u * rise).astype(bf16)
    act_ref[0] = act
    down_part = dot(act, w_down)
    up_grad = (nt(down_grad, w_down) * slope).astype(bf16)
    up_grad_ref[...] = up_grad
    g_bup_ref[...] = jnp.sum(up_grad.astype(f32), axis=0, keepdims=True)
    back_part = nt(up_grad, w_up)

    @pl.when(tile == 0)
    def _():
        down_acc[...] = down_part
        back_acc[...] = back_part

    @pl.when(tile > 0)
    def _():
        down_acc[...] += down_part
        back_acc[...] += back_part

    @pl.when(tile == tiles - 1)
    def _():
        def put(at, values):
            stat_ref[at : at + 1, :] = jnp.sum(values, axis=0, keepdims=True)

        out_grad = cot_ref[...].astype(f32) * live_ref[...]
        down_rows = down_acc[...] + down_bias_ref[...]
        layer_ref[...] = (middle_ref[...] + gate_f * down_rows).astype(bf16)
        put(3, out_grad * down_rows)
        put(4, down_grad.astype(f32))
        hidden_grad = back_acc[...]
        normed = normed_ref[...]
        put(1, hidden_grad)
        put(2, hidden_grad * normed)
        middle_grad = out_grad + norm_back(normed, inv_ref[...], hidden_grad * (1.0 + scale_f))
        grad_ref[...] = middle_grad
        put(0, middle_grad * branch_ref[...])
        branch_grad = (middle_grad * gate_a).astype(bf16)
        two_grad_ref[1] = branch_grad
        put(5, branch_grad.astype(f32))
        put(6, jnp.zeros_like(out_grad))
        put(7, jnp.zeros_like(out_grad))
        att_grad = nt(branch_grad, flat(w_out_ref)).astype(bf16)
        for g in range(groups):
            att_grad_ref[g] = att_grad[:, g * wide : (g + 1) * wide]


def middle(attended, rows, cot, mod, live, biases, stack, parts):
    groups, patches, wide = attended.shape
    hidden_units = biases[2].shape[1]
    devices = stack.shape[0] * parts
    down_rows, up_rows = hidden_units // devices, D // devices
    first_up, first_out = down_rows // up_rows, (down_rows + up_rows * (hidden_units // D)) // up_rows
    span = hidden_units // (2 * parts)
    width = min(512, span)
    tiles = hidden_units // width
    tiles_part = tiles // parts
    per_span = span // width

    def half_at(t):
        block = t // per_span
        return (block % 2, 0, (block // 2) * per_span + t % per_span)

    token_shape = (patches, D)

    def shape(dims, dtype):
        return jax.ShapeDtypeStruct(dims, dtype)

    return pl.pallas_call(
        lambda *refs: middle_kernel(parts, tiles, *refs),
        grid=(tiles,),
        in_specs=[
            full_block(attended.shape), full_block(token_shape), full_block(token_shape),
            full_block((6, D)), full_block((1, 1)), full_block((1, D)), full_block((1, D)),
            pl.BlockSpec((1, width), lambda t: (0, t)),
            pl.BlockSpec((devices // parts, parts, up_rows, D), lambda t: (0, 0, first_out, 0)),
            pl.BlockSpec(
                (devices // parts, parts, up_rows, width),
                lambda t: (0, 0, first_up + t * width // D, t % (D // width)),
            ),
            pl.BlockSpec(
                (width // down_rows, 1, down_rows, D),
                lambda t: (t % tiles_part, t // tiles_part, 0, 0),
            ),
        ],
        out_specs=[
            full_block(token_shape), full_block(token_shape),
            pl.BlockSpec((1, patches, width), half_at),
            pl.BlockSpec((patches, width), lambda t: (0, t)),
            full_block((2,) + token_shape), full_block((2,) + token_shape),
            full_block(attended.shape), full_block((8, D)),
            pl.BlockSpec((1, width), lambda t: (0, t)),
        ],
        out_shape=[
            shape(token_shape, bf16), shape(token_shape, f32),
            shape((2, patches, hidden_units // 2), bf16), shape((patches, hidden_units), bf16),
            shape((2,) + token_shape, bf16), shape((2,) + token_shape, bf16),
            shape(attended.shape, bf16), shape((8, D), f32),
            shape((1, hidden_units), f32),
        ],
        scratch_shapes=[
            pltpu.VMEM(token_shape, bf16), pltpu.VMEM(token_shape, f32),
            pltpu.VMEM(token_shape, f32), pltpu.VMEM(token_shape, f32),
            pltpu.VMEM((patches, 1), f32), pltpu.VMEM(token_shape, bf16),
            pltpu.VMEM(token_shape, f32), pltpu.VMEM(token_shape, f32),
        ],
        compiler_params=pltpu.CompilerParams(vmem_limit_bytes=56 << 20),
        cost_estimate=SHORT,
    )(attended, rows, cot, mod, live, *biases, stack, stack, stack)


def swap(values, axis):
    return lax.ppermute(values, axis, [(0, 1), (1, 0)])


def shifts(values, axis, size):
    me = lax.axis_index(axis)
    found = [(me, values)]
    for shift in range(1, size):
        pairs = [(i, (i + shift) % size) for i in range(size)]
        found.append(((me + size - shift) % size, lax.ppermute(values, axis, pairs)))
    return found


def line_gather(values, axis, size):
    whole = jnp.zeros((size,) + values.shape, values.dtype)
    for place, part in shifts(values, axis, size):
        whole = lax.dynamic_update_index_in_dim(whole, part, place, 0)
    return whole


def line_parts(parts, axis, size):
    me = lax.axis_index(axis)
    kept = lax.dynamic_index_in_dim(parts, me, 0, keepdims=False)
    theirs = [
        lax.dynamic_index_in_dim(parts, (me + shift) % size, 0, keepdims=False)
        for shift in range(1, size)
    ]
    return kept, theirs


def line_move(theirs, axis, size):
    return [
        lax.ppermute(part, axis, [(i, (i + shift) % size) for i in range(size)])
        for shift, part in enumerate(theirs, 1)
    ]


def line_send(parts, axis, size):
    kept, theirs = line_parts(parts, axis, size)
    return kept, line_move(theirs, axis, size)


def add_up(kept, got):
    total = kept.astype(f32)
    for part in got:
        total = total + part.astype(f32)
    return total


def double(sums, rows, between, axis, size):
    me = lax.axis_index(axis)
    height = sums.shape[-2]
    step = 1
    while step < size:
        bit = (me // step) % 2
        both = sums if rows is None else jnp.concatenate([sums, rows], axis=-2)
        both = both.reshape((-1, 2) + both.shape[1:])
        kept = lax.dynamic_index_in_dim(both, bit, 1, keepdims=False)
        theirs = lax.dynamic_index_in_dim(both, 1 - bit, 1, keepdims=False)
        got = lax.ppermute(theirs, axis, [(i, i ^ step) for i in range(size)])
        first = bit == 0
        step *= 2
        if step < size:
            sums = (add_up(kept[:, :height], [got[:, :height]]) + between).astype(bf16)
            if rows is not None:
                rows = in_order(
                    first, kept[:, height:], got[:, height:] + jnp.asarray(between, bf16)
                )
    return kept[0], got[0], first


def in_order(first, own, other):
    return jnp.concatenate([jnp.where(first, own, other), jnp.where(first, other, own)], axis=-2)


def nothing(values):
    return (values[(0,) * values.ndim].astype(f32) > 3e38).astype(f32)


def after(values, earlier):
    return lax.optimization_barrier((values, earlier))[0]


def make_shards(sizes):
    seq = sizes["r"] * sizes["q"]
    dp = sizes["p"] * sizes["c"]
    devices = seq * dp
    heads = H // seq
    wide = heads * HD

    def spread(values, axes):
        return lax.all_to_all(values, axes, 0, 0, tiled=True)

    def shards(
        inputs, cotangent, context, levels, w_qkv, b_qkv, w_out, b_out, w_up, b_up,
        w_down, b_down, w_mod, b_mod,
    ):
        own_frame = lax.axis_index(SEQ)
        core = lax.axis_index("c")
        patches = inputs.shape[1]
        tokens = seq * patches
        own_rows = w_mod.shape[0]

        effective = jnp.where(own_frame < context, 0, levels[:, 0])
        condition = jax.nn.silu(level_embedding(effective, D)).astype(bf16)
        biases = jnp.concatenate([b_qkv, b_out, b_up, b_down, b_mod])
        first = jnp.concatenate(
            [
                condition.reshape(devices, own_rows),
                jnp.broadcast_to(biases, (devices, biases.shape[0])),
            ],
            axis=1,
        )
        first = spread(first, ALL)
        pieces = first[:, :own_rows]
        at = own_rows
        full = []
        for bias in (b_qkv, b_out, b_up, b_down, b_mod):
            size = bias.shape[0]
            full.append(first[:, at : at + size].reshape(-1).astype(f32))
            at += size
        qkv_bias, out_bias, up_bias, down_bias, mod_bias = full
        mod_parts = jnp.dot(pieces, w_mod, preferred_element_type=f32).astype(bf16)
        modulation = jnp.sum(spread(mod_parts, ALL).astype(f32), axis=0) + mod_bias
        scale_attend = modulation[None, D : 2 * D]
        frame_mod = spread(jnp.broadcast_to(modulation[None, : 2 * D], (seq, 2 * D)), SEQ)

        own_qkv = jnp.transpose(w_qkv.reshape(own_rows, 3, seq, wide), (2, 0, 1, 3))
        own_qkv_got = spread(own_qkv.reshape(seq, own_rows, 3 * wide), SEQ)
        own_qkv = line_gather(line_gather(own_qkv_got, "c", sizes["c"]), "p", sizes["p"])
        own_qkv = own_qkv.reshape(D, 3 * wide)

        rows = inputs[0]
        clip = lax.all_gather(rows, SEQ, axis=0, tiled=False)

        def whole(weight):
            return lax.all_gather(weight, ALL, axis=0, tiled=True)

        stack = jnp.concatenate(
            [w_down] + [w_up[:, at : at + D] for at in range(0, w_up.shape[1], D)] + [w_out]
        )
        stack = line_gather(stack + nothing(own_qkv_got).astype(bf16), "p", sizes["p"])
        stack = lax.all_gather(stack, ("c", "r", "q"), axis=0, tiled=False)
        qkv_weight = whole(after(w_qkv, stack))

        own_bias = lax.dynamic_index_in_dim(
            qkv_bias.reshape(3, seq, wide), own_frame, 1, keepdims=False
        ).reshape(1, 3 * wide)
        token = jnp.arange(tokens)
        patch = token % patches
        angles = rope_angles(token // patches, patch // PW, patch % PW, HD)
        cosine, sine = jnp.cos(angles), jnp.sin(angles)
        cosine = jnp.concatenate([cosine, cosine], axis=-1)
        sine = jnp.concatenate([-sine, sine], axis=-1)
        hidden_all, queries, keys, keys_t, values, values_t = project(
            clip, frame_mod.reshape(seq, 2, D), own_qkv, own_bias, cosine, sine, heads
        )
        out_t, attended, lse = attend(queries, keys, values_t, patches)

        attended = spread(attended, SEQ)
        live = (own_frame >= context).astype(f32)[:, None]
        (
            layer_out, middle_grad, activated, up_grad, two_grads, left_halves, attended_grad,
            stats, g_bup,
        ) = middle(
            attended, rows, cotangent[0], modulation.reshape(6, D), live,
            (out_bias[None], down_bias[None], up_bias[None]), stack, sizes["p"],
        )
        gate_attend_grad, shift_feed_grad, scale_feed_grad, gate_feed_grad = (
            stats[i] for i in range(4)
        )
        g_bdown, g_bout = stats[4], stats[5]
        attended_grad = spread(attended_grad, SEQ)

        def both_cores(values):
            mine = lax.dynamic_index_in_dim(values, core, 0, keepdims=False)
            theirs = lax.dynamic_index_in_dim(values, 1 - core, 0, keepdims=False)
            return jnp.concatenate([mine, swap(theirs, "c")])

        two_got = swap(two_grads, "c")
        right = jnp.concatenate([two_grads, two_got], axis=1)
        activated = both_cores(activated)
        left_halves = both_cores(left_halves)
        up_grad = jnp.concatenate([up_grad, swap(up_grad, "c")])

        def by_chip(total):
            half = D // 2
            total = total.astype(bf16).reshape(
                sizes["p"], sizes["r"], sizes["q"], -1, total.shape[1]
            )
            at = [half * block for block in range(total.shape[-1] // half)]
            return [
                [total[..., first : first + half] for first in at[part : part + len(at) // 2]]
                for part in (0, len(at) // 2)
            ]

        g_down = by_chip(outer_sum(activated, right[0]))
        g_up = by_chip(outer_sum(left_halves[:, : D // 2], up_grad))
        g_out = by_chip(outer_sum(left_halves[:, D // 2 :], right[1]))

        groups = []
        for one, two in (g_down, [up + out for up, out in zip(g_up, g_out)]):
            one = jnp.concatenate([jnp.moveaxis(part, 2, 0) for part in one], axis=-2)
            two = jnp.concatenate([jnp.moveaxis(part, 2, 1) for part in two], axis=-2)
            groups.append((line_parts(one, "q", sizes["q"]), line_parts(two, "p", sizes["p"])))

        order = sum(nothing(theirs[0]) for group in groups for _, theirs in group)
        groups = [
            tuple(
                (kept, line_move(theirs, axis, sizes[axis]))
                for (kept, theirs), axis in zip(group, ("q", "p"))
            )
            for group in groups
        ]
        dqkv = attend_back(
            order, queries, keys, keys_t, values, attended_grad, out_t, lse, cosine, sine, patches,
        ).reshape(tokens, 3 * wide)
        qkv_got = spread(dqkv.reshape(seq, patches, 3 * wide), SEQ)
        own_sum = outer_sum(hidden_all, dqkv).astype(bf16).reshape(
            sizes["p"], sizes["c"], sizes["r"], sizes["q"], own_rows, 3 * wide
        )
        own_sum = add_up(*line_send(jnp.moveaxis(own_sum, 1, 0), "c", sizes["c"])).astype(bf16)
        own_sum = add_up(*line_send(own_sum, "p", sizes["p"])).astype(bf16)
        own_kept, own_got = line_send(jnp.moveaxis(own_sum, 1, 0), "q", sizes["q"])
        first_q = lax.axis_index("q") == 0
        own_got = own_got[0]
        own_pair = jnp.concatenate(
            [
                jnp.where(first_q, own_kept, own_got),
                jnp.where(first_q, own_got, own_kept),
                jnp.zeros(own_kept.shape[:-1] + (D - 6 * wide,), bf16),
            ],
            axis=-1,
        )
        qkv_grad = jnp.transpose(
            qkv_got.reshape(seq, patches, 3, wide), (1, 2, 0, 3)
        ).reshape(patches, 3 * D)
        g_bqkv = jnp.sum(qkv_grad.astype(f32), axis=0)
        start_rows = rows.astype(f32)
        hidden_grad = back_dot(qkv_grad, qkv_weight)
        normed, inv_std = layer_norm(start_rows)
        scale_attend_grad = jnp.sum(hidden_grad * normed, axis=0)
        shift_attend_grad = jnp.sum(hidden_grad, axis=0)
        input_grad = middle_grad + norm_back(
            normed, inv_std, hidden_grad * (1.0 + scale_attend)
        )

        mod_grad = jnp.concatenate(
            [
                shift_attend_grad, scale_attend_grad, gate_attend_grad,
                shift_feed_grad, scale_feed_grad, gate_feed_grad,
            ]
        ).astype(bf16)
        last = jnp.concatenate(
            [jnp.broadcast_to(mod_grad, (devices, 6 * D))]
            + [g.astype(bf16).reshape(devices, -1) for g in (g_bqkv, g_bout, g_bup, g_bdown)],
            axis=1,
        )
        thirds = []
        for group, rows_along, before, between in (
            (groups[0], None, sum(nothing(got[0]) for _, got in groups[1]), 0.0),
            (groups[1], own_pair, 0.0, nothing(last)),
        ):
            one, two = ((add_up(*part) + nothing(dqkv)).astype(bf16) for part in group)
            one, two = line_send(one, "p", sizes["p"]), line_send(two, "q", sizes["q"])
            sums = jnp.concatenate([add_up(*one), add_up(*two)], axis=-1) + before
            thirds.append(double(sums.astype(bf16), rows_along, between, "r", sizes["r"]))
        last_got = spread(last, ALL)
        all_mod = last_got[:, : 6 * D]
        g_wmod = outer_sum(pieces, all_mod)
        device = lax.axis_index(ALL)
        g_bmod = jnp.sum(
            lax.dynamic_index_in_dim(
                all_mod.reshape(devices, devices, -1), device, 1, keepdims=False
            ).astype(f32),
            axis=0,
        )
        bias_sums = jnp.sum(last_got[:, 6 * D :].astype(f32), axis=0)
        at = 0
        sums = []
        for bias in (b_qkv, b_out, b_up, b_down):
            sums.append(bias_sums[at : at + bias.shape[0]])
            at += bias.shape[0]
        later = nothing(g_wmod) + nothing(input_grad) + nothing(g_bmod) + nothing(bias_sums)
        (down_kept, down_got, _), (kept, got, first_r) = thirds
        g_wdown = add_up(down_kept, [down_got]) + later
        got = got + later.astype(bf16)
        height = kept.shape[0] - sizes["r"] // 2 * own_rows
        own_all = in_order(first_r, kept[height:], got[height:])
        own_all = own_all.reshape(sizes["r"], own_rows, D)[..., : 6 * wide]
        own_all = own_all.reshape(sizes["r"], own_rows, 2, 3, wide).astype(f32)
        g_wqkv = jnp.transpose(own_all, (1, 3, 0, 2, 4)).reshape(own_rows, 3 * D)
        third = add_up(kept[:height], [got[:height]])
        up_blocks = third[:-own_rows].reshape(-1, own_rows, D)
        g_wup = jnp.concatenate(
            [
                up_blocks[block, :, part * D // 2 : (part + 1) * D // 2]
                for part in range(2)
                for block in range(up_blocks.shape[0])
            ],
            axis=1,
        )
        g_wout = third[-own_rows:]
        return (
            layer_out[None].astype(bf16), input_grad[None].astype(bf16),
            g_wqkv, sums[0], g_wout, sums[1], g_wup, sums[2], g_wdown, sums[3], g_wmod, g_bmod,
        )

    return shards


def solution(mesh):
    dp, seq = mesh.shape["dp"], mesh.shape["seq"]
    sizes = {"p": dp // 2, "c": 2, "r": seq // 2, "q": 2}
    fine = Mesh(mesh.devices.reshape(dp // 2, 2, seq // 2, 2), ALL)
    rows = P(("p", "c"), SEQ, None)
    weight, bias = P(ALL, None), P(ALL)
    pairs = (weight, bias)
    return jax.shard_map(
        make_shards(sizes),
        mesh=fine,
        in_specs=(rows, rows, P(("p", "c")), P(("p", "c"), SEQ)) + pairs * 5,
        out_specs=(rows, rows) + pairs * 5,
        check_vma=False,
    )
```

```python
import math

import jax
import jax.numpy as jnp
from jax import lax
from jax.experimental import pallas as pl
from jax.experimental.pallas import tpu as pltpu
from jax.sharding import Mesh, PartitionSpec as P

D = 1024
H = 16
HD = 64
PW = 16
EPS = 1e-06

ALL = ("p", "c", "r", "q")
SEQ = ("r", "q")
bf16 = jnp.bfloat16
SHORT = pl.CostEstimate(flops=1, bytes_accessed=1, transcendentals=0)
f32 = jnp.float32


def layer_norm(values):
    row_mean = jnp.mean(values, axis=-1, keepdims=True)
    centred = values - row_mean
    inv_std = lax.rsqrt(jnp.mean(centred * centred, axis=-1, keepdims=True) + EPS)
    return (centred * inv_std, inv_std)


def norm_back(normed, inv_std, normed_grad):
    first_mean = jnp.mean(normed_grad, axis=-1, keepdims=True)
    second_mean = jnp.mean(normed_grad * normed, axis=-1, keepdims=True)
    return inv_std * (normed_grad - first_mean - normed * second_mean)


def level_embedding(effective, width):
    half_width = width // 2
    frequency = jnp.exp(
        -math.log(10000.0) * jnp.arange(half_width).astype(f32) / half_width
    )
    angles = effective.astype(f32)[..., None] * frequency
    return jnp.concatenate([jnp.cos(angles), jnp.sin(angles)], axis=-1)


def rope_angles(frame_pos, row_pos, column_pos, head_width):
    pair_count = head_width // 2
    time_pairs = head_width // 8
    space_pairs = 3 * head_width // 16
    pair_index = jnp.arange(pair_count)
    axis_pick = jnp.where(
        pair_index < time_pairs, 0, jnp.where(pair_index < time_pairs + space_pairs, 1, 2)
    )
    local_rank = jnp.where(
        axis_pick == 0,
        pair_index,
        jnp.where(axis_pick == 1, pair_index - time_pairs, pair_index - time_pairs - space_pairs),
    )
    group_size = jnp.where(axis_pick == 0, time_pairs, space_pairs)
    frequency = jnp.exp(-math.log(10000.0) * local_rank.astype(f32) / group_size.astype(f32))
    position = jnp.where(
        axis_pick == 0,
        frame_pos[:, None],
        jnp.where(axis_pick == 1, row_pos[:, None], column_pos[:, None]),
    )
    return position.astype(f32) * frequency


def outer_sum(left, right):
    return lax.dot_general(
        left, right, (((0,), (0,)), ((), ())), preferred_element_type=f32
    )


def back_dot(grads, weight):
    return lax.dot_general(
        grads, weight, (((1,), (1,)), ((), ())), preferred_element_type=f32
    )


def nt(a, b):
    return lax.dot_general(a, b, (((1,), (1,)), ((), ())), preferred_element_type=f32)


def dot(a, b):
    return jnp.dot(a, b, preferred_element_type=f32)


def full_block(shape):
    return pl.BlockSpec(shape, lambda *_: (0,) * len(shape))


def project_kernel(
    heads, rows_ref, mod_ref, weight_ref, bias_ref, cos_ref, sin_ref,
    hidden_ref, q_ref, k_ref, kt_ref, v_ref, vt_ref,
):
    normed, _ = layer_norm(rows_ref[0].astype(f32))
    hidden = (normed * (1.0 + mod_ref[0, 1:2, :]) + mod_ref[0, 0:1, :]).astype(bf16)
    hidden_ref[...] = hidden
    made = dot(hidden, weight_ref[...]) + bias_ref[...]
    wide = heads * HD
    cosine, sine = cos_ref[...], sin_ref[...]

    def turn(values):
        half = HD // 2
        turned = jnp.concatenate([values[:, half:], values[:, :half]], axis=1)
        return values * cosine + turned * sine

    for h in range(heads):
        at = h * HD
        query = turn(made[:, at : at + HD]).astype(bf16).astype(f32)
        key = turn(made[:, wide + at : wide + at + HD])
        value = made[:, 2 * wide + at : 2 * wide + at + HD]
        q_ref[h] = (query * (1.0 / math.sqrt(HD))).astype(bf16)
        k_ref[h] = key.astype(bf16)
        kt_ref[h] = jnp.transpose(key).astype(bf16)
        v_ref[h] = value.astype(bf16)
        vt_ref[h] = jnp.transpose(value).astype(bf16)


def project(clip, frame_mod, weight, bias, cosine, sine, heads):
    frames, block, _ = clip.shape
    tokens = frames * block
    wide = heads * HD
    tall = pl.BlockSpec((heads, block, HD), lambda i: (0, i, 0))
    flat = pl.BlockSpec((heads, HD, block), lambda i: (0, 0, i))
    tall_shape = jax.ShapeDtypeStruct((heads, tokens, HD), bf16)
    flat_shape = jax.ShapeDtypeStruct((heads, HD, tokens), bf16)
    return pl.pallas_call(
        lambda *refs: project_kernel(heads, *refs),
        grid=(frames,),
        in_specs=[
            pl.BlockSpec((1, block, D), lambda i: (i, 0, 0)),
            pl.BlockSpec((1, 2, D), lambda i: (i, 0, 0)),
            full_block((D, 3 * wide)),
            full_block((1, 3 * wide)),
            pl.BlockSpec((block, HD), lambda i: (i, 0)),
            pl.BlockSpec((block, HD), lambda i: (i, 0)),
        ],
        out_specs=[pl.BlockSpec((block, D), lambda i: (i, 0)), tall, tall, flat, tall, flat],
        out_shape=[
            jax.ShapeDtypeStruct((tokens, D), bf16),
            tall_shape, tall_shape, flat_shape, tall_shape, flat_shape,
        ],
        compiler_params=pltpu.CompilerParams(vmem_limit_bytes=40 << 20),
        cost_estimate=SHORT,
    )(clip, frame_mod, weight, bias, cosine, sine)


def attend_kernel(
    block, heads, frames, q_ref, k_ref, vt_ref, ot_ref, out_ref, lse_ref, score_ref
):
    count = frames + 1

    def pair_step(first, _):
        second = frames - 1 - first

        def place(n):
            early = n <= first
            query_frame = jnp.where(early, first, second)
            key_frame = jnp.where(early, n, n - first - 1)
            return (
                early,
                pl.ds(pl.multiple_of(query_frame * block, block), block),
                pl.ds(pl.multiple_of(key_frame * block, block), block),
            )

        for h in range(heads):
            tops = []
            for n in range(count):
                _, rows, keys = place(n)
                scores = nt(k_ref[h, keys, :], q_ref[h, rows, :])
                score_ref[h, n] = scores
                tops.append(jnp.max(scores, axis=0, keepdims=True))
            low = jnp.full((1, block), -1e30, f32)
            top_a, top_b = low, low
            for n in range(count):
                early = n <= first
                top_a = jnp.maximum(top_a, jnp.where(early, tops[n], low))
                top_b = jnp.maximum(top_b, jnp.where(early, low, tops[n]))
            zero = jnp.zeros((1, block), f32)
            sum_a, sum_b = zero, zero
            acc_a = jnp.zeros((HD, block), f32)
            acc_b = acc_a
            for n in range(count):
                early, _, keys = place(n)
                weights = jnp.exp(score_ref[h, n] - jnp.where(early, top_a, top_b))
                part_sum = jnp.sum(weights, axis=0, keepdims=True)
                part = dot(vt_ref[h, :, keys], weights.astype(bf16))
                if n == 0:
                    sum_a, acc_a = part_sum, part
                elif n > (frames - 1) // 2:
                    sum_b, acc_b = sum_b + part_sum, acc_b + part
                else:
                    sum_a = sum_a + jnp.where(early, part_sum, 0.0)
                    sum_b = sum_b + jnp.where(early, 0.0, part_sum)
                    acc_a = acc_a + jnp.where(early, part, 0.0)
                    acc_b = acc_b + jnp.where(early, 0.0, part)
            for frame, top, total, acc in (
                (first, top_a, sum_a, acc_a), (second, top_b, sum_b, acc_b),
            ):
                rows = pl.ds(pl.multiple_of(frame * block, block), block)
                done = acc / total
                ot_ref[h, :, rows] = done
                out_ref[frame, :, h * HD : (h + 1) * HD] = jnp.transpose(done).astype(bf16)
                lse_ref[h, :, rows] = top + jnp.log(total)
        return 0

    lax.fori_loop(0, frames // 2, pair_step, 0)


def attend(queries, keys, values_t, block):
    heads, tokens, _ = queries.shape
    frames = tokens // block
    return pl.pallas_call(
        lambda *refs: attend_kernel(block, heads, frames, *refs),
        out_shape=[
            jax.ShapeDtypeStruct((heads, HD, tokens), f32),
            jax.ShapeDtypeStruct((frames, block, heads * HD), bf16),
            jax.ShapeDtypeStruct((heads, 1, tokens), f32),
        ],
        scratch_shapes=[pltpu.VMEM((heads, frames + 1, block, block), f32)],
        compiler_params=pltpu.CompilerParams(vmem_limit_bytes=40 << 20),
        cost_estimate=SHORT,
    )(queries, keys, values_t)


def attend_back_kernel(
    block, heads, frames, _, q_ref, k_ref, kt_ref, v_ref, do_ref, ot_ref, lse_ref, cos_ref, sin_ref,
    out_ref, dqt_ref, delta_ref,
):
    dqt_ref[...] = jnp.zeros_like(dqt_ref)
    wide = heads * HD
    scale = 1.0 / math.sqrt(HD)
    for i in range(frames):
        rows = slice(i * block, (i + 1) * block)
        for h in range(heads):
            grad_t = jnp.transpose(do_ref[i, :, h * HD : (h + 1) * HD].astype(f32))
            delta_ref[h, :, rows] = jnp.sum(grad_t * ot_ref[h, :, rows], axis=0, keepdims=True)

    def back(values, rows):
        half = HD // 2
        turned = jnp.concatenate([values[:, half:], values[:, :half]], axis=1)
        return (values * cos_ref[rows, :] - turned * sin_ref[rows, :]).astype(bf16)

    def pair_step(first, _):
        second = frames - 1 - first
        for h in range(heads):
            zero = jnp.zeros((block, HD), f32)
            dk_a, dv_a, dk_b, dv_b = zero, zero, zero, zero
            for n in range(frames + 1):
                early = n < frames - first
                query_frame = jnp.where(early, first + n, n - 1)
                key_frame = jnp.where(early, first, second)
                rows = pl.ds(pl.multiple_of(query_frame * block, block), block)
                keys = pl.ds(pl.multiple_of(key_frame * block, block), block)
                query = q_ref[h, rows, :]
                grad = do_ref[query_frame, :, h * HD : (h + 1) * HD]
                probs = jnp.exp(nt(k_ref[h, keys, :], query) - lse_ref[h, :, rows])
                prob_grad = nt(v_ref[h, keys, :], grad)
                score_grad = (probs * (prob_grad - delta_ref[h, :, rows])).astype(bf16)
                dv = dot(probs.astype(bf16), grad)
                dk = dot(score_grad, query)
                dqt_ref[h, :, rows] += dot(kt_ref[h, :, keys], score_grad)
                if n < frames - (frames - 1) // 2:
                    dk_a, dv_a = dk_a + dk, dv_a + dv
                elif n == frames:
                    dk_b, dv_b = dk_b + dk, dv_b + dv
                else:
                    dk_a = dk_a + jnp.where(early, dk, 0.0)
                    dv_a = dv_a + jnp.where(early, dv, 0.0)
                    dk_b = dk_b + jnp.where(early, 0.0, dk)
                    dv_b = dv_b + jnp.where(early, 0.0, dv)
            for frame, dk, dv in ((first, dk_a, dv_a), (second, dk_b, dv_b)):
                rows = pl.ds(pl.multiple_of(frame * block, block), block)
                at = wide + h * HD
                out_ref[frame, :, at : at + HD] = back(dk, rows)
                out_ref[frame, :, wide + at : wide + at + HD] = dv.astype(bf16)
        return 0

    lax.fori_loop(0, frames // 2, pair_step, 0)
    for i in range(frames):
        rows = slice(i * block, (i + 1) * block)
        for h in range(heads):
            out_ref[i, :, h * HD : (h + 1) * HD] = back(
                jnp.transpose(dqt_ref[h, :, rows]) * scale, rows
            )


def attend_back(order, queries, keys, keys_t, values, grad, out_t, lse, cosine, sine, block):
    heads, tokens, _ = queries.shape
    frames = tokens // block
    return pl.pallas_call(
        lambda *refs: attend_back_kernel(block, heads, frames, *refs),
        out_shape=jax.ShapeDtypeStruct((frames, block, 3 * heads * HD), bf16),
        scratch_shapes=[
            pltpu.VMEM((heads, HD, tokens), f32),
            pltpu.VMEM((heads, 1, tokens), f32),
        ],
        compiler_params=pltpu.CompilerParams(vmem_limit_bytes=48 << 20),
        cost_estimate=SHORT,
    )(order.reshape(1, 1), queries, keys, keys_t, values, grad, out_t, lse, cosine, sine)


def middle_kernel(
    parts, tiles, att_ref, in_ref, cot_ref, mod_ref, live_ref, out_bias_ref, down_bias_ref,
    up_bias_ref, w_out_ref, w_up_ref, w_down_ref,
    layer_ref, grad_ref, act_ref, up_grad_ref, two_grad_ref, half_ref,
    att_grad_ref, stat_ref, g_bup_ref,
    att_all, branch_ref, middle_ref, normed_ref, inv_ref, hidden_ref, down_acc, back_acc,
):
    tile = pl.program_id(0)
    gate_a, shift_f, scale_f, gate_f = (mod_ref[i : i + 1, :] for i in (2, 3, 4, 5))
    groups, _, wide = att_ref.shape
    span = D // (2 * parts)

    def flat(ref):
        last = ref.shape[-1]
        return jnp.concatenate(
            [ref[:, p].reshape(-1, last) for p in range(ref.shape[1])], axis=0
        )

    def halves(start, values):
        for p in range(parts):
            for c in range(2):
                at = (2 * p + c) * span
                to = start + p * span
                half_ref[c, :, to : to + span] = values[:, at : at + span]

    @pl.when(tile == 0)
    def _():
        for g in range(groups):
            att_all[:, g * wide : (g + 1) * wide] = att_ref[g]
        attended = att_all[...]
        halves(D // 2, attended)
        branch = dot(attended, flat(w_out_ref)) + out_bias_ref[...]
        branch_ref[...] = branch
        middle = in_ref[...].astype(f32) + gate_a * branch
        middle_ref[...] = middle
        normed, inv_std = layer_norm(middle)
        normed_ref[...] = normed
        inv_ref[...] = inv_std
        hidden = (normed * (1.0 + scale_f) + shift_f).astype(bf16)
        hidden_ref[...] = hidden
        halves(0, hidden)
        two_grad_ref[0] = (cot_ref[...].astype(f32) * live_ref[...] * gate_f).astype(bf16)

    hidden = hidden_ref[...]
    down_grad = two_grad_ref[0]
    w_up, w_down = flat(w_up_ref), flat(w_down_ref)
    u = dot(hidden, w_up) + up_bias_ref[...]
    scale = math.sqrt(2.0 / math.pi)
    square = u * u
    bend = jnp.tanh(scale * (u + 0.044715 * (u * square)))
    rise = 0.5 * (1.0 + bend)
    slope = rise + (0.5 * scale) * u * (1.0 - bend * bend) * (1.0 + (3.0 * 0.044715) * square)
    act = (u * rise).astype(bf16)
    act_ref[0] = act
    down_part = dot(act, w_down)
    up_grad = (nt(down_grad, w_down) * slope).astype(bf16)
    up_grad_ref[...] = up_grad
    g_bup_ref[...] = jnp.sum(up_grad.astype(f32), axis=0, keepdims=True)
    back_part = nt(up_grad, w_up)

    @pl.when(tile == 0)
    def _():
        down_acc[...] = down_part
        back_acc[...] = back_part

    @pl.when(tile > 0)
    def _():
        down_acc[...] += down_part
        back_acc[...] += back_part

    @pl.when(tile == tiles - 1)
    def _():
        def put(at, values):
            stat_ref[at : at + 1, :] = jnp.sum(values, axis=0, keepdims=True)

        out_grad = cot_ref[...].astype(f32) * live_ref[...]
        down_rows = down_acc[...] + down_bias_ref[...]
        layer_ref[...] = (middle_ref[...] + gate_f * down_rows).astype(bf16)
        put(3, out_grad * down_rows)
        put(4, down_grad.astype(f32))
        hidden_grad = back_acc[...]
        normed = normed_ref[...]
        put(1, hidden_grad)
        put(2, hidden_grad * normed)
        middle_grad = out_grad + norm_back(normed, inv_ref[...], hidden_grad * (1.0 + scale_f))
        grad_ref[...] = middle_grad
        put(0, middle_grad * branch_ref[...])
        branch_grad = (middle_grad * gate_a).astype(bf16)
        two_grad_ref[1] = branch_grad
        put(5, branch_grad.astype(f32))
        put(6, jnp.zeros_like(out_grad))
        put(7, jnp.zeros_like(out_grad))
        att_grad = nt(branch_grad, flat(w_out_ref)).astype(bf16)
        for g in range(groups):
            att_grad_ref[g] = att_grad[:, g * wide : (g + 1) * wide]


def middle(attended, rows, cot, mod, live, biases, stack, parts):
    groups, patches, wide = attended.shape
    hidden_units = biases[2].shape[1]
    devices = stack.shape[0] * parts
    down_rows, up_rows = hidden_units // devices, D // devices
    first_up, first_out = down_rows // up_rows, (down_rows + up_rows * (hidden_units // D)) // up_rows
    span = hidden_units // (2 * parts)
    width = min(512, span)
    tiles = hidden_units // width
    tiles_part = tiles // parts
    per_span = span // width

    def half_at(t):
        block = t // per_span
        return (block % 2, 0, (block // 2) * per_span + t % per_span)

    token_shape = (patches, D)

    def shape(dims, dtype):
        return jax.ShapeDtypeStruct(dims, dtype)

    return pl.pallas_call(
        lambda *refs: middle_kernel(parts, tiles, *refs),
        grid=(tiles,),
        in_specs=[
            full_block(attended.shape), full_block(token_shape), full_block(token_shape),
            full_block((6, D)), full_block((1, 1)), full_block((1, D)), full_block((1, D)),
            pl.BlockSpec((1, width), lambda t: (0, t)),
            pl.BlockSpec((devices // parts, parts, up_rows, D), lambda t: (0, 0, first_out, 0)),
            pl.BlockSpec(
                (devices // parts, parts, up_rows, width),
                lambda t: (0, 0, first_up + t * width // D, t % (D // width)),
            ),
            pl.BlockSpec(
                (width // down_rows, 1, down_rows, D),
                lambda t: (t % tiles_part, t // tiles_part, 0, 0),
            ),
        ],
        out_specs=[
            full_block(token_shape), full_block(token_shape),
            pl.BlockSpec((1, patches, width), half_at),
            pl.BlockSpec((patches, width), lambda t: (0, t)),
            full_block((2,) + token_shape), full_block((2,) + token_shape),
            full_block(attended.shape), full_block((8, D)),
            pl.BlockSpec((1, width), lambda t: (0, t)),
        ],
        out_shape=[
            shape(token_shape, bf16), shape(token_shape, f32),
            shape((2, patches, hidden_units // 2), bf16), shape((patches, hidden_units), bf16),
            shape((2,) + token_shape, bf16), shape((2,) + token_shape, bf16),
            shape(attended.shape, bf16), shape((8, D), f32),
            shape((1, hidden_units), f32),
        ],
        scratch_shapes=[
            pltpu.VMEM(token_shape, bf16), pltpu.VMEM(token_shape, f32),
            pltpu.VMEM(token_shape, f32), pltpu.VMEM(token_shape, f32),
            pltpu.VMEM((patches, 1), f32), pltpu.VMEM(token_shape, bf16),
            pltpu.VMEM(token_shape, f32), pltpu.VMEM(token_shape, f32),
        ],
        compiler_params=pltpu.CompilerParams(vmem_limit_bytes=56 << 20),
        cost_estimate=SHORT,
    )(attended, rows, cot, mod, live, *biases, stack, stack, stack)


def swap(values, axis):
    return lax.ppermute(values, axis, [(0, 1), (1, 0)])


def shifts(values, axis, size):
    me = lax.axis_index(axis)
    found = [(me, values)]
    for shift in range(1, size):
        pairs = [(i, (i + shift) % size) for i in range(size)]
        found.append(((me + size - shift) % size, lax.ppermute(values, axis, pairs)))
    return found


def line_gather(values, axis, size):
    whole = jnp.zeros((size,) + values.shape, values.dtype)
    for place, part in shifts(values, axis, size):
        whole = lax.dynamic_update_index_in_dim(whole, part, place, 0)
    return whole


def line_parts(parts, axis, size):
    me = lax.axis_index(axis)
    kept = lax.dynamic_index_in_dim(parts, me, 0, keepdims=False)
    theirs = [
        lax.dynamic_index_in_dim(parts, (me + shift) % size, 0, keepdims=False)
        for shift in range(1, size)
    ]
    return kept, theirs


def line_move(theirs, axis, size):
    return [
        lax.ppermute(part, axis, [(i, (i + shift) % size) for i in range(size)])
        for shift, part in enumerate(theirs, 1)
    ]


def line_send(parts, axis, size):
    kept, theirs = line_parts(parts, axis, size)
    return kept, line_move(theirs, axis, size)


def add_up(kept, got):
    total = kept.astype(f32)
    for part in got:
        total = total + part.astype(f32)
    return total


def double(sums, rows, between, axis, size):
    me = lax.axis_index(axis)
    height = sums.shape[-2]
    step = 1
    while step < size:
        bit = (me // step) % 2
        both = sums if rows is None else jnp.concatenate([sums, rows], axis=-2)
        both = both.reshape((-1, 2) + both.shape[1:])
        kept = lax.dynamic_index_in_dim(both, bit, 1, keepdims=False)
        theirs = lax.dynamic_index_in_dim(both, 1 - bit, 1, keepdims=False)
        got = lax.ppermute(theirs, axis, [(i, i ^ step) for i in range(size)])
        first = bit == 0
        step *= 2
        if step < size:
            sums = (add_up(kept[:, :height], [got[:, :height]]) + between).astype(bf16)
            if rows is not None:
                rows = in_order(
                    first, kept[:, height:], got[:, height:] + jnp.asarray(between, bf16)
                )
    return kept[0], got[0], first


def in_order(first, own, other):
    return jnp.concatenate([jnp.where(first, own, other), jnp.where(first, other, own)], axis=-2)


def nothing(values):
    return (values[(0,) * values.ndim].astype(f32) > 3e38).astype(f32)


def after(values, earlier):
    return lax.optimization_barrier((values, earlier))[0]


def make_shards(sizes):
    seq = sizes["r"] * sizes["q"]
    dp = sizes["p"] * sizes["c"]
    devices = seq * dp
    heads = H // seq
    wide = heads * HD

    def spread(values, axes):
        return lax.all_to_all(values, axes, 0, 0, tiled=True)

    def shards(
        inputs, cotangent, context, levels, w_qkv, b_qkv, w_out, b_out, w_up, b_up,
        w_down, b_down, w_mod, b_mod,
    ):
        own_frame = lax.axis_index(SEQ)
        core = lax.axis_index("c")
        patches = inputs.shape[1]
        tokens = seq * patches
        own_rows = w_mod.shape[0]

        effective = jnp.where(own_frame < context, 0, levels[:, 0])
        condition = jax.nn.silu(level_embedding(effective, D)).astype(bf16)
        biases = jnp.concatenate([b_qkv, b_out, b_up, b_down, b_mod])
        first = jnp.concatenate(
            [
                condition.reshape(devices, own_rows),
                jnp.broadcast_to(biases, (devices, biases.shape[0])),
            ],
            axis=1,
        )
        first = spread(first, ALL)
        pieces = first[:, :own_rows]
        at = own_rows
        full = []
        for bias in (b_qkv, b_out, b_up, b_down, b_mod):
            size = bias.shape[0]
            full.append(first[:, at : at + size].reshape(-1).astype(f32))
            at += size
        qkv_bias, out_bias, up_bias, down_bias, mod_bias = full
        mod_parts = jnp.dot(pieces, w_mod, preferred_element_type=f32).astype(bf16)
        modulation = jnp.sum(spread(mod_parts, ALL).astype(f32), axis=0) + mod_bias
        scale_attend = modulation[None, D : 2 * D]
        frame_mod = spread(jnp.broadcast_to(modulation[None, : 2 * D], (seq, 2 * D)), SEQ)

        own_qkv = jnp.transpose(w_qkv.reshape(own_rows, 3, seq, wide), (2, 0, 1, 3))
        own_qkv_got = spread(own_qkv.reshape(seq, own_rows, 3 * wide), SEQ)
        own_qkv = line_gather(line_gather(own_qkv_got, "c", sizes["c"]), "p", sizes["p"])
        own_qkv = own_qkv.reshape(D, 3 * wide)

        rows = inputs[0]
        clip = lax.all_gather(rows, SEQ, axis=0, tiled=False)

        def whole(weight):
            return lax.all_gather(weight, ALL, axis=0, tiled=True)

        stack = jnp.concatenate(
            [w_down] + [w_up[:, at : at + D] for at in range(0, w_up.shape[1], D)] + [w_out]
        )
        stack = line_gather(stack + nothing(own_qkv_got).astype(bf16), "p", sizes["p"])
        stack = lax.all_gather(stack, ("c", "r", "q"), axis=0, tiled=False)
        qkv_weight = whole(after(w_qkv, stack))

        own_bias = lax.dynamic_index_in_dim(
            qkv_bias.reshape(3, seq, wide), own_frame, 1, keepdims=False
        ).reshape(1, 3 * wide)
        token = jnp.arange(tokens)
        patch = token % patches
        angles = rope_angles(token // patches, patch // PW, patch % PW, HD)
        cosine, sine = jnp.cos(angles), jnp.sin(angles)
        cosine = jnp.concatenate([cosine, cosine], axis=-1)
        sine = jnp.concatenate([-sine, sine], axis=-1)
        hidden_all, queries, keys, keys_t, values, values_t = project(
            clip, frame_mod.reshape(seq, 2, D), own_qkv, own_bias, cosine, sine, heads
        )
        out_t, attended, lse = attend(queries, keys, values_t, patches)

        attended = spread(attended, SEQ)
        live = (own_frame >= context).astype(f32)[:, None]
        (
            layer_out, middle_grad, activated, up_grad, two_grads, left_halves, attended_grad,
            stats, g_bup,
        ) = middle(
            attended, rows, cotangent[0], modulation.reshape(6, D), live,
            (out_bias[None], down_bias[None], up_bias[None]), stack, sizes["p"],
        )
        gate_attend_grad, shift_feed_grad, scale_feed_grad, gate_feed_grad = (
            stats[i] for i in range(4)
        )
        g_bdown, g_bout = stats[4], stats[5]
        attended_grad = spread(attended_grad, SEQ)

        def both_cores(values):
            mine = lax.dynamic_index_in_dim(values, core, 0, keepdims=False)
            theirs = lax.dynamic_index_in_dim(values, 1 - core, 0, keepdims=False)
            return jnp.concatenate([mine, swap(theirs, "c")])

        two_got = swap(two_grads, "c")
        right = jnp.concatenate([two_grads, two_got], axis=1)
        activated = both_cores(activated)
        left_halves = both_cores(left_halves)
        up_grad = jnp.concatenate([up_grad, swap(up_grad, "c")])

        def by_chip(total):
            half = D // 2
            total = total.astype(bf16).reshape(
                sizes["p"], sizes["r"], sizes["q"], -1, total.shape[1]
            )
            at = [half * block for block in range(total.shape[-1] // half)]
            return [
                [total[..., first : first + half] for first in at[part : part + len(at) // 2]]
                for part in (0, len(at) // 2)
            ]

        g_down = by_chip(outer_sum(activated, right[0]))
        g_up = by_chip(outer_sum(left_halves[:, : D // 2], up_grad))
        g_out = by_chip(outer_sum(left_halves[:, D // 2 :], right[1]))

        groups = []
        for one, two in (g_down, [up + out for up, out in zip(g_up, g_out)]):
            one = jnp.concatenate([jnp.moveaxis(part, 2, 0) for part in one], axis=-2)
            two = jnp.concatenate([jnp.moveaxis(part, 2, 1) for part in two], axis=-2)
            groups.append((line_parts(one, "q", sizes["q"]), line_parts(two, "p", sizes["p"])))

        order = sum(nothing(theirs[0]) for group in groups for _, theirs in group)
        groups = [
            tuple(
                (kept, line_move(theirs, axis, sizes[axis]))
                for (kept, theirs), axis in zip(group, ("q", "p"))
            )
            for group in groups
        ]
        dqkv = attend_back(
            order, queries, keys, keys_t, values, attended_grad, out_t, lse, cosine, sine, patches,
        ).reshape(tokens, 3 * wide)
        qkv_got = spread(dqkv.reshape(seq, patches, 3 * wide), SEQ)
        own_sum = outer_sum(hidden_all, dqkv).astype(bf16).reshape(
            sizes["p"], sizes["c"], sizes["r"], sizes["q"], own_rows, 3 * wide
        )
        along = sum(nothing(got[0]) for _, got in groups[1])
        own_sum = add_up(*line_send(jnp.moveaxis(own_sum, 1, 0), "c", sizes["c"])) + along
        own_sum = own_sum.astype(bf16)
        def chip_step(group, before):
            one, two = (
                (add_up(*part) + nothing(dqkv) + before).astype(bf16) for part in group
            )
            return line_send(one, "p", sizes["p"]), line_send(two, "q", sizes["q"])

        own_send = line_send(own_sum, "p", sizes["p"])
        chip_steps = [chip_step(group, along) for group in groups]
        own_sum = add_up(*own_send) + sum(nothing(got[0]) for _, got in chip_steps[0])
        own_sum = own_sum.astype(bf16)
        own_kept, own_got = line_send(jnp.moveaxis(own_sum, 1, 0), "q", sizes["q"])
        first_q = lax.axis_index("q") == 0
        own_got = own_got[0]
        own_pair = jnp.concatenate(
            [
                jnp.where(first_q, own_kept, own_got),
                jnp.where(first_q, own_got, own_kept),
                jnp.zeros(own_kept.shape[:-1] + (D - 6 * wide,), bf16),
            ],
            axis=-1,
        )
        qkv_grad = jnp.transpose(
            qkv_got.reshape(seq, patches, 3, wide), (1, 2, 0, 3)
        ).reshape(patches, 3 * D)
        g_bqkv = jnp.sum(qkv_grad.astype(f32), axis=0)
        start_rows = rows.astype(f32)
        hidden_grad = back_dot(qkv_grad, qkv_weight)
        normed, inv_std = layer_norm(start_rows)
        scale_attend_grad = jnp.sum(hidden_grad * normed, axis=0)
        shift_attend_grad = jnp.sum(hidden_grad, axis=0)
        input_grad = middle_grad + norm_back(
            normed, inv_std, hidden_grad * (1.0 + scale_attend)
        )

        mod_grad = jnp.concatenate(
            [
                shift_attend_grad, scale_attend_grad, gate_attend_grad,
                shift_feed_grad, scale_feed_grad, gate_feed_grad,
            ]
        ).astype(bf16)
        last = jnp.concatenate(
            [jnp.broadcast_to(mod_grad, (devices, 6 * D))]
            + [g.astype(bf16).reshape(devices, -1) for g in (g_bqkv, g_bout, g_bup, g_bdown)],
            axis=1,
        )
        thirds = []
        for (one, two), rows_along in zip(chip_steps, (None, own_pair)):
            sums = jnp.concatenate([add_up(*one), add_up(*two)], axis=-1)
            sums = sums.astype(bf16)
            thirds.append(double(sums, rows_along, nothing(last), "r", sizes["r"]))
        last_got = spread(last, ALL)
        all_mod = last_got[:, : 6 * D]
        g_wmod = outer_sum(pieces, all_mod)
        device = lax.axis_index(ALL)
        g_bmod = jnp.sum(
            lax.dynamic_index_in_dim(
                all_mod.reshape(devices, devices, -1), device, 1, keepdims=False
            ).astype(f32),
            axis=0,
        )
        bias_sums = jnp.sum(last_got[:, 6 * D :].astype(f32), axis=0)
        at = 0
        sums = []
        for bias in (b_qkv, b_out, b_up, b_down):
            sums.append(bias_sums[at : at + bias.shape[0]])
            at += bias.shape[0]
        later = nothing(g_wmod) + nothing(input_grad) + nothing(g_bmod) + nothing(bias_sums)
        (down_kept, down_got, _), (kept, got, first_r) = thirds
        g_wdown = add_up(down_kept, [down_got]) + later
        got = got + later.astype(bf16)
        height = kept.shape[0] - sizes["r"] // 2 * own_rows
        own_all = in_order(first_r, kept[height:], got[height:])
        own_all = own_all.reshape(sizes["r"], own_rows, D)[..., : 6 * wide]
        own_all = own_all.reshape(sizes["r"], own_rows, 2, 3, wide).astype(f32)
        g_wqkv = jnp.transpose(own_all, (1, 3, 0, 2, 4)).reshape(own_rows, 3 * D)
        third = add_up(kept[:height], [got[:height]])
        up_blocks = third[:-own_rows].reshape(-1, own_rows, D)
        g_wup = jnp.concatenate(
            [
                up_blocks[block, :, part * D // 2 : (part + 1) * D // 2]
                for part in range(2)
                for block in range(up_blocks.shape[0])
            ],
            axis=1,
        )
        g_wout = third[-own_rows:]
        return (
            layer_out[None].astype(bf16), input_grad[None].astype(bf16),
            g_wqkv, sums[0], g_wout, sums[1], g_wup, sums[2], g_wdown, sums[3], g_wmod, g_bmod,
        )

    return shards


def solution(mesh):
    dp, seq = mesh.shape["dp"], mesh.shape["seq"]
    sizes = {"p": dp // 2, "c": 2, "r": seq // 2, "q": 2}
    fine = Mesh(mesh.devices.reshape(dp // 2, 2, seq // 2, 2), ALL)
    rows = P(("p", "c"), SEQ, None)
    weight, bias = P(ALL, None), P(ALL)
    pairs = (weight, bias)
    return jax.shard_map(
        make_shards(sizes),
        mesh=fine,
        in_specs=(rows, rows, P(("p", "c")), P(("p", "c"), SEQ)) + pairs * 5,
        out_specs=(rows, rows) + pairs * 5,
        check_vma=False,
    )
```
